1024 devices in a mesh: clus: 128 (over z, y), rhs: 8 (over x, core).
Axes of the slice: x: 4, y: 8, z: 16, core: 2. Of those that a mesh axis runs over, the one named last changes fastest.
Arguments:
- points: float32 [3, 262144], P(None, 'clus'), may hold values from 0 to 1
- rhs_cols: float32 [32, 262144], P('rhs', 'clus'), may hold values from -6 to 6
- leaf_basis: float32 [1024, 64, 256], P('clus', 'rhs'), may hold values from -0.375 to 0.375
- leaf_nodes: float32 [1024, 3, 64], P('clus'), may hold values from 0 to 1
- leaf_transfer: float32 [1024, 64, 64], P('clus'), may hold values from -0.25 to 0.25
- near_mask: int32 [1024, 9], P('clus'), may hold values 0 or 1
- top_transfer: float32 [252, 64, 64], replicated, may hold values from -0.5 to 0.5
- top_nodes: float32 [254, 3, 64], replicated, may hold values from 0 to 1
Outputs:
- product: float32 [32, 262144], P('rhs', 'clus')
The draws below stay inside these ranges and needn't reach their ends.
All inputs are finite; a program needn't handle non-finite values. No bound on the sum of `near_mask` on one device may be relied on, other than what follows from the above.
Results may differ from the reference program's by a relative error of at most 0.0003.
Values sent between devices are 32-bit elements; how exact they have to be, the bound alone decides.
A program may use at most 64 MiB of HBM per device.

```python
import jax
import jax.numpy as jnp
from jax import lax

LEAF = 256
R = 64
NRHS = 32
HALO = 4
LEAVES_DEV = 8
LEAVES = 1024
POINTS = 262144
SLOTS = 9
LEVELS = 7
TOP_NODES = 252
ALL_NODES = 254
N_CLUS = 128


def set_ends(array, stream_key, low, high):
    shape = array.shape
    place = [jax.random.randint(jax.random.fold_in(stream_key, axis), (), 0, shape[axis]) for axis in range(len(shape))]
    array = array.at[tuple(place)].set(low)
    longest = shape.index(max(shape))
    place[longest] = (place[longest] + 1) % shape[longest]
    return array.at[tuple(place)].set(high)


def levels(stream_key, shape, pieces, smallest, largest):
    def one(axis_at, parts):
        steps = jax.random.uniform(jax.random.fold_in(jax.random.fold_in(stream_key, 6), axis_at), (parts,), jnp.float32, smallest / len(pieces), largest / len(pieces))
        return jnp.repeat(jnp.exp(steps), shape[axis_at] // parts).reshape((-1,) + (1,) * (len(shape) - axis_at - 1))

    loudness = one(*pieces[0])
    for cut in pieces[1:]:
        loudness = loudness * one(*cut)
    return loudness


def scatter_about(key, dims, deviation, reach, pieces=(), held_as=jnp.bfloat16):
    loudness = levels(key, dims, pieces, -0.22, 0.18) if pieces else 1.0
    result = jax.random.normal(key, dims, jnp.float32) * deviation * loudness
    return jnp.minimum(jnp.maximum(result, -reach), reach).astype(held_as)


def setup_inputs(seed: int = 0) -> dict:
    seeds = jax.random.split(jax.random.key(seed), 9)
    return {
        "points": jnp.clip(1.0 * jax.random.uniform(seeds[0], (3, POINTS), jnp.float32) ** levels(seeds[0], (3, POINTS), ((1, 128),), -0.2, 0.2), 0.0, 1.0),
        "rhs_cols": scatter_about(seeds[1], (NRHS, POINTS), 1.0, 6.0, ((0, 8), (1, 128)), jnp.float32),
        "leaf_basis": scatter_about(seeds[2], (LEAVES, R, LEAF), LEAF ** -0.5, 0.375, ((0, 128), (1, 8)), jnp.float32),
        "leaf_nodes": jnp.clip(1.0 * jax.random.uniform(seeds[3], (LEAVES, 3, R), jnp.float32) ** levels(seeds[3], (LEAVES, 3, R), ((0, 128),), -0.2, 0.2), 0.0, 1.0),
        "leaf_transfer": scatter_about(seeds[4], (LEAVES, R, R), (R * LEAVES_DEV) ** -0.5, 0.25, ((0, 128),), jnp.float32),
        "near_mask": set_ends((jax.random.randint(seeds[5], (LEAVES, SLOTS), 0, 3) < 1).astype(jnp.int32), jax.random.fold_in(seeds[5], 1), 0, 1),
        "top_transfer": scatter_about(seeds[6], (TOP_NODES, R, R), (2 * R) ** -0.5, 0.5, (), jnp.float32),
        "top_nodes": jnp.clip(jax.random.uniform(seeds[7], (ALL_NODES, 3, R), jnp.float32, 0.0, 1.0), 0.0, 1.0),
    }


AMPLITUDE = 0.2
INV_SCALE = 1.0 / (2.0 * 0.15 * 0.15)
HIGHEST = lax.Precision.HIGHEST


def kernel_block(targets, sources):
    first = targets[..., 0, :, None] - sources[..., 0, None, :]
    second = targets[..., 1, :, None] - sources[..., 1, None, :]
    third = targets[..., 2, :, None] - sources[..., 2, None, :]
    dist = first * first + second * second + third * third
    return AMPLITUDE * jnp.exp(-dist * INV_SCALE)


def reference(points, rhs_cols, leaf_basis, leaf_nodes, leaf_transfer, near_mask, top_transfer, top_nodes):
    width = HALO * LEAF
    pad_points = jnp.pad(points, ((0, 0), (width, width)))
    pad_rhs = jnp.pad(rhs_cols, ((0, 0), (width, width)))
    slot_ids = jnp.arange(SLOTS, dtype=jnp.int32)
    weights = jnp.where(slot_ids[None, :] == HALO, 1, near_mask).astype(jnp.float32)
    column_weights = jnp.repeat(weights, LEAF, axis=1)

    def near_leaf(index):
        start = (index * LEAF).astype(jnp.int32)
        win_points = lax.dynamic_slice_in_dim(pad_points, start, SLOTS * LEAF, 1)
        win_rhs = lax.dynamic_slice_in_dim(pad_rhs, start, SLOTS * LEAF, 1)
        own = lax.dynamic_slice_in_dim(points, start, LEAF, 1)
        block = kernel_block(own, win_points) * column_weights[index][None, :]
        return jnp.dot(win_rhs, block.T, precision=HIGHEST)

    near = lax.map(near_leaf, jnp.arange(LEAVES, dtype=jnp.int32))
    rhs_leaf = rhs_cols.reshape(NRHS, LEAVES, LEAF)
    moments = jnp.einsum('grl,cgl->grc', leaf_basis, rhs_leaf, precision=HIGHEST)
    pad_moments = jnp.pad(moments, ((HALO, HALO), (0, 0), (0, 0)))
    pad_nodes = jnp.pad(leaf_nodes, ((HALO, HALO), (0, 0), (0, 0)))
    local_far = jnp.zeros((LEAVES, R, NRHS), jnp.float32)
    for slot in range(SLOTS):
        coupling = kernel_block(leaf_nodes, pad_nodes[slot:slot + LEAVES])
        term = jnp.einsum('gab,gbc->gac', coupling, pad_moments[slot:slot + LEAVES], precision=HIGHEST)
        local_far = local_far + (1.0 - weights[:, slot])[:, None, None] * term
    lifted = jnp.einsum('gab,gbc->gac', leaf_transfer, moments, precision=HIGHEST)
    upward = [jnp.sum(lifted.reshape(N_CLUS, LEAVES_DEV, R, NRHS), axis=1)]
    for level in range(LEVELS - 1):
        count = N_CLUS >> level
        offset = 2 * N_CLUS - 2 * count
        terms = jnp.einsum('nab,nbc->nac', top_transfer[offset:offset + count], upward[level], precision=HIGHEST)
        upward.append(terms[0::2] + terms[1::2])
    couples = []
    for level in range(LEVELS):
        count = N_CLUS >> level
        offset = 2 * N_CLUS - 2 * count
        nodes = top_nodes[offset:offset + count]
        partner_nodes = nodes.reshape(count // 2, 2, 3, R)[:, ::-1].reshape(count, 3, R)
        partner_moments = upward[level].reshape(count // 2, 2, R, NRHS)[:, ::-1].reshape(count, R, NRHS)
        coupling = kernel_block(nodes, partner_nodes)
        couples.append(jnp.einsum('nab,nbc->nac', coupling, partner_moments, precision=HIGHEST))
    downward = couples[LEVELS - 1]
    for level in range(LEVELS - 2, -1, -1):
        count = N_CLUS >> level
        offset = 2 * N_CLUS - 2 * count
        parent = jnp.repeat(downward, 2, axis=0)
        downward = couples[level] + jnp.einsum('nba,nbc->nac', top_transfer[offset:offset + count], parent, precision=HIGHEST)
    spread = jnp.repeat(downward, LEAVES_DEV, axis=0)
    local = local_far + jnp.einsum('gba,gbc->gac', leaf_transfer, spread, precision=HIGHEST)
    far = jnp.einsum('grl,grc->cgl', leaf_basis, local, precision=HIGHEST)
    product = jnp.transpose(near, (1, 0, 2)) + far
    return product.reshape(NRHS, POINTS)
```

```python
import functools
import math

import jax
import jax.numpy as jnp
from jax import lax
from jax.experimental import pallas as pl
from jax.experimental.pallas import tpu as pltpu
from jax.sharding import PartitionSpec as P

AMPLITUDE = 0.2
INV_SCALE = 1.0 / (2.0 * 0.15 * 0.15)
COORD = math.sqrt(INV_SCALE * math.log2(math.e))
LOG_AMP = math.log2(AMPLITUDE)

F32 = jnp.float32
BF16 = jnp.bfloat16
MESH = pl.DeviceIdType.MESH

NN = (((1,), (0,)), ((), ()))
NT = (((1,), (1,)), ((), ()))
TN = (((0,), (0,)), ((), ()))

Y = 8
Z = 16
R = 64
LEAF = 256
LV = 8
COLS = 4
REACH = 4
SLOTS = 9
EXT = LV + 2 * REACH
HALO = REACH * LEAF


def split(x):
    hi = x.astype(BF16)
    return hi, (x - hi.astype(F32)).astype(BF16)


def dot(a, b, dims):
    return lax.dot_general(a, b, dims, preferred_element_type=F32)


def mm(a, b, dims):
    ah, al = split(a)
    bh, bl = split(b)
    return dot(ah, bh, dims) + (dot(ah, bl, dims) + dot(al, bh, dims))


def mtn(a, b):
    ah, al = split(a)
    bh, bl = split(b)
    return dot(jnp.concatenate([ah, ah, al], 0), jnp.concatenate([bh, bl, bh], 0), TN)


def rows8(x):
    hi = x.astype(BF16).astype(F32)
    return jnp.concatenate([hi, x - hi], 0)


def fold8(x):
    return x[0:COLS] + x[COLS : 2 * COLS]


def columns(seg):
    return jnp.concatenate([seg, jnp.zeros((5, seg.shape[1]), F32)], 0).T


def gauss(cols, rows):
    d0 = cols[0] - rows[0]
    d1 = cols[1] - rows[1]
    d2 = cols[2] - rows[2]
    return jnp.exp2(LOG_AMP - (d0 * d0 + d1 * d1 + d2 * d2))


def body(
    points, rhs, basis_in, nodes_in, lt_in, mask_in, top_t, top_n,
    out,
    pts, cols_s, lhs8, rh, nodes, mom, basis, lt, mask, wn,
    t0, t1, t2, t3, t4, t5, tn, upy, upz, m0, mz, ltc, qc, wd, pre, far8,
    lsem, bs_s, bs_r, hs_s, hs_r, ms_s, ms_r, ys_s, ys_r, zs_s, zs_r,
):
    c = lax.axis_index("clus")
    r = lax.axis_index("rhs")
    z = c // Y
    y = lax.rem(c, Y)
    n_clus = Y * Z
    nxt = lax.rem(c + 1, n_clus)
    prv = lax.rem(c + n_clus - 1, n_clus)

    r_peers = [(c, lax.rem(r + k, 8)) for k in range(1, 8)]
    y_peers = [(z * Y + lax.rem(y + k, Y), r) for k in range(1, Y)]
    z_peers = [(lax.rem(z + k, Z) * Y + y, r) for k in range(1, Z)]
    everyone = r_peers + y_peers + z_peers + [(nxt, r), (prv, r)]
    barrier = pltpu.get_barrier_semaphore()
    for p in everyone:
        pl.semaphore_signal(barrier, inc=1, device_id=p, device_id_type=MESH)

    own = pl.ds(HALO, LV * LEAF)
    loads = [
        (basis_in, basis.at[r]),
        (rhs, rh.at[:, own]),
        (lt_in, lt),
        (points, pts.at[:, own]),
        (nodes_in, nodes.at[pl.ds(REACH, LV)]),
        (mask_in, mask),
        (top_t.at[pl.ds(Y * z, Y)], t0),
        (top_t.at[pl.ds(128 + 4 * z, 4)], t1),
        (top_t.at[pl.ds(192 + 2 * z, 2)], t2),
        (top_t.at[pl.ds(224, 16)], t3),
        (top_t.at[pl.ds(240, 8)], t4),
        (top_t.at[pl.ds(248, 4)], t5),
    ]
    for b in range(7):
        off = 256 - 2 * (128 >> b)
        loads.append((top_n.at[pl.ds(off + 2 * (c >> (b + 1)), 2)], tn.at[b]))
    local = []
    for i, (src, dst) in enumerate(loads):
        cp = pltpu.make_async_copy(src, dst, lsem.at[i])
        cp.start()
        local.append(cp)

    pl.semaphore_wait(barrier, len(everyone))

    def remote(src, dst, s, q, to):
        cp = pltpu.make_async_remote_copy(
            src_ref=src, dst_ref=dst, send_sem=s, recv_sem=q, device_id=to, device_id_type=MESH
        )
        cp.start()
        return cp

    sent_b = [remote(basis_in, basis.at[r], bs_s.at[i], bs_r.at[i], p) for i, p in enumerate(r_peers)]
    right = pl.ds(LV * LEAF - HALO, HALO)
    left = pl.ds(0, HALO)
    to_left = pl.ds(0, HALO)
    to_right = pl.ds(HALO + LV * LEAF, HALO)
    sent_h = [
        remote(points.at[:, right], pts.at[:, to_left], hs_s.at[0], hs_r.at[0], (nxt, r)),
        remote(points.at[:, left], pts.at[:, to_right], hs_s.at[1], hs_r.at[1], (prv, r)),
        remote(rhs.at[:, right], rh.at[:, to_left], hs_s.at[2], hs_r.at[2], (nxt, r)),
        remote(rhs.at[:, left], rh.at[:, to_right], hs_s.at[3], hs_r.at[3], (prv, r)),
        remote(nodes_in.at[pl.ds(LV - REACH, REACH)], nodes.at[pl.ds(0, REACH)], hs_s.at[4], hs_r.at[4], (nxt, r)),
        remote(nodes_in.at[pl.ds(0, REACH)], nodes.at[pl.ds(REACH + LV, REACH)], hs_s.at[5], hs_r.at[5], (prv, r)),
    ]

    for cp in local:
        cp.wait()
    ltc[...] = jnp.concatenate([lt[g] for g in range(LV)], 1)
    q1 = [mm(t1[k], jnp.concatenate([t0[2 * k], t0[2 * k + 1]], 1), NN) for k in range(4)]
    qc[...] = jnp.concatenate(
        [mm(t2[k], jnp.concatenate([q1[2 * k], q1[2 * k + 1]], 1), NN) for k in range(2)], 1
    )
    path = [t0[y], t1[y >> 1], t2[y >> 2], t3[z], t4[z >> 1], t5[z >> 2]]
    e = None
    g_b = []
    for b in range(7):
        mine = lax.rem(c >> b, 2)
        mn = tn[b, pl.ds(mine, 1)][0] * COORD
        sn = tn[b, pl.ds(1 - mine, 1)][0] * COORD
        sc = columns(jnp.concatenate([sn, sn], 1))[0:R]
        s_t = gauss([sc[:, k : k + 1] for k in range(3)], [mn[k : k + 1] for k in range(3)])
        if b == 0:
            g_b.append(s_t)
        else:
            e = path[0] if b == 1 else mm(path[b - 1], e, NN)
            g_b.append(mm(s_t, e, NN))
    zero = jnp.zeros((R, R), F32)
    m0[y] = zero
    m0[y ^ 1] = g_b[0]
    s1 = (y >> 1) ^ 1
    for k in range(2):
        m0[2 * s1 + k] = mtn(t0[2 * s1 + k], g_b[1])
    s2 = (y >> 2) ^ 1
    for k in range(2):
        half = mtn(t1[2 * s2 + k], g_b[2])
        for j in range(2):
            m0[4 * s2 + 2 * k + j] = mtn(t0[4 * s2 + 2 * k + j], half)
    mz[z] = zero
    mz[z ^ 1] = g_b[3]
    s4 = (z >> 1) ^ 1
    for k in range(2):
        mz[2 * s4 + k] = mtn(t3[2 * s4 + k], g_b[4])
    s5 = (z >> 2) ^ 1
    for k in range(2):
        half = mtn(t4[2 * s5 + k], g_b[5])
        for j in range(2):
            mz[4 * s5 + 2 * k + j] = mtn(t3[4 * s5 + 2 * k + j], half)
    s6 = (z >> 3) ^ 1
    for i in range(2):
        top = mtn(t5[2 * s6 + i], g_b[6])
        for k in range(2):
            half = mtn(t4[4 * s6 + 2 * i + k], top)
            for j in range(2):
                mz[8 * s6 + 4 * i + 2 * k + j] = mtn(t3[8 * s6 + 4 * i + 2 * k + j], half)

    for cp in sent_b:
        cp.wait_recv()
    parts = []
    for g in range(LV):
        bg = basis[:, g].reshape(R, LEAF)
        parts.append(mm(rh[:, HALO + g * LEAF : HALO + (g + 1) * LEAF], bg, NT))
    moments = jnp.concatenate(parts, 1)
    mom[:, REACH * R : (REACH + LV) * R] = moments
    upy[y] = mm(moments, ltc[...], NT)
    sent_y = [remote(upy.at[y], upy.at[y], ys_s.at[i], ys_r.at[i], p) for i, p in enumerate(y_peers)]
    sent_m = [
        remote(mom.at[:, pl.ds(LV * R, REACH * R)], mom.at[:, pl.ds(0, REACH * R)], ms_s.at[0], ms_r.at[0], (nxt, r)),
        remote(mom.at[:, pl.ds(REACH * R, REACH * R)], mom.at[:, pl.ds((REACH + LV) * R, REACH * R)], ms_s.at[1], ms_r.at[1], (prv, r)),
    ]
    for g in range(LV):
        wd[:, g * LEAF : (g + 1) * LEAF] = mm(lt[g], basis[:, g].reshape(R, LEAF), NN)

    for cp in sent_y:
        cp.wait_recv()
    flat_y = jnp.concatenate([upy[k] for k in range(Y)], 1)
    upz[z] = mm(flat_y, qc[...], NT)
    sent_z = [remote(upz.at[z], upz.at[z], zs_s.at[i], zs_r.at[i], p) for i, p in enumerate(z_peers)]

    pre[...] = mm(flat_y, m0[...].reshape(Y * R, R), NN)

    for cp in sent_h:
        cp.wait_recv()
    lane = lax.broadcasted_iota(jnp.int32, (LV, SLOTS), 1)
    row = lax.broadcasted_iota(jnp.int32, (LV, SLOTS), 0)
    place = c * LV + row + lane - REACH
    valid = jnp.where((place >= 0) & (place < n_clus * LV), 1.0, 0.0).astype(F32)
    w = jnp.where(lane == REACH, 1.0, mask[...].astype(F32))
    wn[...] = w * valid
    wf = (1.0 - w) * valid

    skew = []
    for g in range(LV):
        piece = [wf[g : g + 1]]
        if g > 0:
            piece.insert(0, jnp.zeros((1, g), F32))
        if g < LV - 1:
            piece.append(jnp.zeros((1, LV - 1 - g), F32))
        skew.append(jnp.concatenate(piece, 1))
    skewed = jnp.concatenate(skew, 0)
    spread = jnp.where(
        lax.broadcasted_iota(jnp.int32, (LV, LV * R), 1) // R == lax.broadcasted_iota(jnp.int32, (LV, LV * R), 0),
        1.0, 0.0,
    ).astype(F32)
    far_w = dot(skewed, spread, TN)

    for cp in sent_m:
        cp.wait_recv()
    m8 = rows8(mom[...]).astype(BF16)
    flat_n = jnp.concatenate([nodes[l] for l in range(EXT)], 1) * COORD
    mine_n = flat_n[:, REACH * R : (REACH + LV) * R]
    targets = [mine_n[k : k + 1] for k in range(3)]
    acc = jnp.zeros((2 * COLS, LV * R), F32)
    for q in range(EXT // 4):
        hs, ls = [], []
        for p in range(2):
            cc = columns(flat_n[:, (2 * q + p) * 128 : (2 * q + p + 1) * 128])
            for u in range(2):
                l = 4 * q + 2 * p + u
                part = cc[u * R : (u + 1) * R]
                block = gauss([part[:, k : k + 1] for k in range(3)], targets) * far_w[l : l + 1]
                h, lo = split(block)
                hs.append(h)
                ls.append(lo)
        a = m8[:, q * 256 : (q + 1) * 256]
        acc = acc + dot(a, jnp.concatenate(hs, 0), NN) + dot(a, jnp.concatenate(ls, 0), NN)
    local_far = fold8(acc)
    for g in range(LV):
        far8[:, g * LEAF : (g + 1) * LEAF] = mm(
            local_far[:, g * R : (g + 1) * R], basis[:, g].reshape(R, LEAF), NN
        )

    lhs8[...] = rows8(rh[...])

    def prepare(l, _):
        for h in range(2):
            at = pl.multiple_of(l * LEAF + h * 128, 128)
            cc = columns(pts[:, pl.ds(at, 128)] * COORD)
            for k in range(3):
                cols_s[l, k, h * 128 : (h + 1) * 128] = jnp.broadcast_to(cc[:, k : k + 1], (128, 128))
        return 0

    lax.fori_loop(0, EXT, prepare, 0)

    def near(g, _):
        at = pl.multiple_of(HALO + g * LEAF, LEAF)
        tg = pts[:, pl.ds(at, LEAF)] * COORD
        wrow = wn[pl.ds(g, 1), :]
        accs = [jnp.zeros((2 * COLS, 128), F32) for _ in range(2)]
        for s in range(SLOTS):
            l = g + s
            a = (lhs8[:, pl.ds(pl.multiple_of(l * LEAF, LEAF), LEAF)] * wrow[:, s : s + 1]).astype(BF16)
            for h in range(2):
                k_hi, k_lo = split(
                    gauss(
                        [cols_s[l, k] for k in range(3)],
                        [tg[k : k + 1, h * 128 : (h + 1) * 128] for k in range(3)],
                    )
                )
                accs[h] = accs[h] + dot(a, k_hi, NN) + dot(a, k_lo, NN)
        to = pl.multiple_of(g * LEAF, LEAF)
        far8[:, pl.ds(to, LEAF)] = far8[:, pl.ds(to, LEAF)] + fold8(jnp.concatenate(accs, 1))
        return 0

    lax.fori_loop(0, LV, near, 0)

    for cp in sent_z:
        cp.wait_recv()
    flat_z = jnp.concatenate([upz[k] for k in range(Z)], 1)
    down = mm(flat_z, mz[...].reshape(Z * R, R), NN) + pre[...]
    out[...] = mm(down, wd[...], NN) + far8[...]

    for cp in sent_b + sent_h + sent_m + sent_y + sent_z:
        cp.wait_send()


def on_device(points, rhs_cols, leaf_basis, leaf_nodes, leaf_transfer, near_mask, top_transfer, top_nodes):
    any_space = pl.BlockSpec(memory_space=pl.ANY)
    dma = pltpu.SemaphoreType.DMA
    v = lambda *s: pltpu.VMEM(s, F32)
    return pl.pallas_call(
        body,
        out_shape=jax.ShapeDtypeStruct(rhs_cols.shape, F32),
        in_specs=[any_space] * 8,
        out_specs=pl.BlockSpec(memory_space=pltpu.VMEM),
        scratch_shapes=[
            v(3, EXT * LEAF),
            v(EXT, 3, LEAF, 128),
            v(2 * COLS, EXT * LEAF),
            v(COLS, EXT * LEAF),
            v(EXT, 3, R),
            v(COLS, EXT * R),
            v(8, LV, 8, LEAF),
            v(LV, R, R),
            pltpu.VMEM((LV, SLOTS), jnp.int32),
            v(LV, SLOTS),
            v(8, R, R), v(4, R, R), v(2, R, R), v(16, R, R), v(8, R, R), v(4, R, R),
            v(7, 2, 3, R),
            v(Y, COLS, R),
            v(Z, COLS, R),
            v(Y, R, R), v(Z, R, R),
            v(R, LV * R), v(R, Y * R),
            v(R, LV * LEAF),
            v(COLS, R),
            v(COLS, LV * LEAF),
            dma((19,)),
            dma((7,)), dma((7,)), dma((6,)), dma((6,)), dma((2,)), dma((2,)),
            dma((Y - 1,)), dma((Y - 1,)), dma((Z - 1,)), dma((Z - 1,)),
        ],
        compiler_params=pltpu.CompilerParams(
            collective_id=0, has_side_effects=True, vmem_limit_bytes=48 * 1024 * 1024
        ),
        cost_estimate=pl.CostEstimate(flops=10**9, bytes_accessed=4 * 10**6, transcendentals=5 * 10**6),
    )(points, rhs_cols, leaf_basis, leaf_nodes, leaf_transfer, near_mask, top_transfer, top_nodes)


def solution(mesh):
    return jax.shard_map(
        on_device,
        mesh=mesh,
        in_specs=(
            P(None, "clus"),
            P("rhs", "clus"),
            P("clus", "rhs", None),
            P("clus", None, None),
            P("clus", None, None),
            P("clus", None),
            P(),
            P(),
        ),
        out_specs=P("rhs", "clus"),
        check_vma=False,
    )
```

```python
import functools
import math

import jax
import jax.numpy as jnp
from jax import lax
from jax.experimental import pallas as pl
from jax.experimental.pallas import tpu as pltpu
from jax.sharding import PartitionSpec as P

AMPLITUDE = 0.2
INV_SCALE = 1.0 / (2.0 * 0.15 * 0.15)
COORD = math.sqrt(INV_SCALE * math.log2(math.e))
LOG_AMP = math.log2(AMPLITUDE)

F32 = jnp.float32
BF16 = jnp.bfloat16
MESH = pl.DeviceIdType.MESH

NN = (((1,), (0,)), ((), ()))
NT = (((1,), (1,)), ((), ()))
TN = (((0,), (0,)), ((), ()))

Y = 8
Z = 16
R = 64
LEAF = 256
LV = 8
COLS = 4
REACH = 4
SLOTS = 9
EXT = LV + 2 * REACH
HALO = REACH * LEAF


def split(x):
    hi = x.astype(BF16)
    return hi, (x - hi.astype(F32)).astype(BF16)


def dot(a, b, dims):
    return lax.dot_general(a, b, dims, preferred_element_type=F32)


def mm(a, b, dims):
    ah, al = split(a)
    bh, bl = split(b)
    return dot(ah, bh, dims) + (dot(ah, bl, dims) + dot(al, bh, dims))


def mtn(a, b):
    ah, al = split(a)
    bh, bl = split(b)
    return dot(jnp.concatenate([ah, ah, al], 0), jnp.concatenate([bh, bl, bh], 0), TN)


def rows8(x):
    hi = x.astype(BF16).astype(F32)
    return jnp.concatenate([hi, x - hi], 0)


def fold8(x):
    return x[0:COLS] + x[COLS : 2 * COLS]


def columns(seg):
    return jnp.concatenate([seg, jnp.zeros((5, seg.shape[1]), F32)], 0).T


def gauss(cols, rows):
    d0 = cols[0] - rows[0]
    d1 = cols[1] - rows[1]
    d2 = cols[2] - rows[2]
    return jnp.exp2(LOG_AMP - (d0 * d0 + d1 * d1 + d2 * d2))


class Refs:
    pass


def extract(t):
    def turn(a, _):
        slab = t.slab[a]
        low = slab[:, 0:128].T
        high = jnp.concatenate([slab[:, 128:], jnp.zeros((R, 256 - t.n_top), F32)], 1).T
        t.turned[pl.ds(pl.multiple_of(a * 256, 256), 128), :] = low
        t.turned[pl.ds(pl.multiple_of(a * 256 + 128, 128), 128), :] = high
        return 0

    lax.fori_loop(0, R, turn, 0, unroll=4)
    for k in range(3):
        x = t.nslab[k] * COORD
        t.nturned[k, 0:128] = x[:, 0:128].T
        t.nturned[k, 128:256] = jnp.concatenate([x[:, 128:], jnp.zeros((R, 2), F32)], 1).T


def operators(t):
    z, y, c = t.z, t.y, t.c

    def top(n):
        return t.turned[pl.ds(n, R, stride=256), :]

    t0 = lambda k: top(Y * z + k)
    t1 = lambda k: top(128 + 4 * z + k)
    t2 = lambda k: top(192 + 2 * z + k)
    t3 = lambda k: top(224 + k)
    t4 = lambda k: top(240 + k)
    t5 = lambda k: top(248 + k)
    q1 = [mm(t1(k), jnp.concatenate([t0(2 * k), t0(2 * k + 1)], 1), NN) for k in range(4)]
    t.qc[...] = jnp.concatenate(
        [mm(t2(k), jnp.concatenate([q1[2 * k], q1[2 * k + 1]], 1), NN) for k in range(2)], 1
    )
    path = [t0(y), t1(y >> 1), t2(y >> 2), t3(z), t4(z >> 1), t5(z >> 2)]
    e = None
    g_b = []
    for b in range(7):
        off = 256 - 2 * (128 >> b)
        at = off + (c >> b)
        sib = off + ((c >> b) ^ 1)
        mn = [t.nturned[k, pl.ds(at, 1)] for k in range(3)]
        sn = jnp.concatenate([t.nturned[k, pl.ds(sib, 1)] for k in range(3)], 0)
        sc = columns(jnp.concatenate([sn, sn], 1))[0:R]
        s_t = gauss([sc[:, k : k + 1] for k in range(3)], mn)
        if b == 0:
            g_b.append(s_t)
        else:
            e = path[0] if b == 1 else mm(path[b - 1], e, NN)
            g_b.append(mm(s_t, e, NN))
    zero = jnp.zeros((R, R), F32)
    m0, mz = t.m0, t.mz
    m0[y] = zero
    m0[y ^ 1] = g_b[0]
    s1 = (y >> 1) ^ 1
    for k in range(2):
        m0[2 * s1 + k] = mtn(t0(2 * s1 + k), g_b[1])
    s2 = (y >> 2) ^ 1
    for k in range(2):
        half = mtn(t1(2 * s2 + k), g_b[2])
        for j in range(2):
            m0[4 * s2 + 2 * k + j] = mtn(t0(4 * s2 + 2 * k + j), half)
    mz[z] = zero
    mz[z ^ 1] = g_b[3]
    s4 = (z >> 1) ^ 1
    for k in range(2):
        mz[2 * s4 + k] = mtn(t3(2 * s4 + k), g_b[4])
    s5 = (z >> 2) ^ 1
    for k in range(2):
        half = mtn(t4(2 * s5 + k), g_b[5])
        for j in range(2):
            mz[4 * s5 + 2 * k + j] = mtn(t3(4 * s5 + 2 * k + j), half)
    s6 = (z >> 3) ^ 1
    for i in range(2):
        up = mtn(t5(2 * s6 + i), g_b[6])
        for k in range(2):
            half = mtn(t4(4 * s6 + 2 * i + k), up)
            for j in range(2):
                mz[8 * s6 + 4 * i + 2 * k + j] = mtn(t3(8 * s6 + 4 * i + 2 * k + j), half)


def leaf_basis_of(t, g):
    return t.basis[:, g].reshape(R, LEAF)


def gather_transfers(t):
    t.ltc[...] = jnp.concatenate([t.lt[g] for g in range(LV)], 1)


def expand(t):
    parts = []
    for g in range(LV):
        parts.append(mm(t.rh[:, HALO + g * LEAF : HALO + (g + 1) * LEAF], leaf_basis_of(t, g), NT))
    moments = jnp.concatenate(parts, 1)
    t.mom[:, REACH * R : (REACH + LV) * R] = moments
    t.upy[t.y] = mm(moments, t.ltc[...], NT)


def lift_basis(t):
    for g in range(LV):
        t.wd[:, g * LEAF : (g + 1) * LEAF] = mm(t.lt[g], leaf_basis_of(t, g), NN)


def weights(t):
    lane = lax.broadcasted_iota(jnp.int32, (LV, SLOTS), 1)
    row = lax.broadcasted_iota(jnp.int32, (LV, SLOTS), 0)
    place = t.c * LV + row + lane - REACH
    valid = jnp.where((place >= 0) & (place < Y * Z * LV), 1.0, 0.0).astype(F32)
    w = jnp.where(lane == REACH, 1.0, t.mask[...].astype(F32))
    t.wn[...] = w * valid
    wf = (1.0 - w) * valid
    skew = []
    for g in range(LV):
        piece = [wf[g : g + 1]]
        if g > 0:
            piece.insert(0, jnp.zeros((1, g), F32))
        if g < LV - 1:
            piece.append(jnp.zeros((1, LV - 1 - g), F32))
        skew.append(jnp.concatenate(piece, 1))
    skewed = jnp.concatenate(skew, 0)
    spread = jnp.where(
        lax.broadcasted_iota(jnp.int32, (LV, LV * R), 1) // R == lax.broadcasted_iota(jnp.int32, (LV, LV * R), 0),
        1.0, 0.0,
    ).astype(F32)
    t.fw[...] = dot(skewed, spread, TN)


def leaf_far(t):
    m8 = rows8(t.mom[...]).astype(BF16)
    flat = []
    for k in range(3):
        rows = [t.nodes[0, k, l : l + 1] for l in range(LV - REACH, LV)]
        rows += [t.nodes[1, k, l : l + 1] for l in range(LV)]
        rows += [t.nodes[2, k, l : l + 1] for l in range(REACH)]
        flat.append(jnp.concatenate(rows, 1))
    flat_n = jnp.concatenate(flat, 0) * COORD
    mine_n = flat_n[:, REACH * R : (REACH + LV) * R]
    targets = [mine_n[k : k + 1] for k in range(3)]
    far_w = t.fw[...]
    acc = jnp.zeros((2 * COLS, LV * R), F32)
    for q in range(EXT // 4):
        hs, ls = [], []
        for p in range(2):
            cc = columns(flat_n[:, (2 * q + p) * 128 : (2 * q + p + 1) * 128])
            for u in range(2):
                l = 4 * q + 2 * p + u
                part = cc[u * R : (u + 1) * R]
                block = gauss([part[:, k : k + 1] for k in range(3)], targets) * far_w[l : l + 1]
                h, lo = split(block)
                hs.append(h)
                ls.append(lo)
        a = m8[:, q * 256 : (q + 1) * 256]
        acc = acc + dot(a, jnp.concatenate(hs, 0), NN) + dot(a, jnp.concatenate(ls, 0), NN)
    local_far = fold8(acc)
    for g in range(LV):
        cut = slice(g * LEAF, (g + 1) * LEAF)
        t.far8[:, cut] = t.far8[:, cut] + mm(local_far[:, g * R : (g + 1) * R], leaf_basis_of(t, g), NN)


def source_columns(t, first, count):
    def prepare(l, _):
        for h in range(2):
            at = pl.multiple_of(l * LEAF + h * 128, 128)
            cc = columns(t.pts[:, pl.ds(at, 128)] * COORD)
            for k in range(3):
                t.cols_s[l, k, h * 128 : (h + 1) * 128] = jnp.broadcast_to(cc[:, k : k + 1], (128, 128))
        at = pl.multiple_of(l * LEAF, LEAF)
        t.lhs8[:, pl.ds(at, LEAF)] = rows8(t.rh[:, pl.ds(at, LEAF)])
        return 0

    lax.fori_loop(first, first + count, prepare, 0)


def near(t, first, count):
    def leaf(g, _):
        at = pl.multiple_of(HALO + g * LEAF, LEAF)
        tg = t.pts[:, pl.ds(at, LEAF)] * COORD
        wrow = t.wn[pl.ds(g, 1), :]
        accs = [jnp.zeros((2 * COLS, 128), F32) for _ in range(2)]
        for s in range(SLOTS):
            l = g + s
            a = (t.lhs8[:, pl.ds(pl.multiple_of(l * LEAF, LEAF), LEAF)] * wrow[:, s : s + 1]).astype(BF16)
            for h in range(2):
                k_hi, k_lo = split(
                    gauss(
                        [t.cols_s[l, k] for k in range(3)],
                        [tg[k : k + 1, h * 128 : (h + 1) * 128] for k in range(3)],
                    )
                )
                accs[h] = accs[h] + dot(a, k_hi, NN) + dot(a, k_lo, NN)
        to = pl.multiple_of(g * LEAF, LEAF)
        t.far8[:, pl.ds(to, LEAF)] = fold8(jnp.concatenate(accs, 1))
        return 0

    lax.fori_loop(first, first + count, leaf, 0)


def level_three(t):
    flat_y = jnp.concatenate([t.upy[k] for k in range(Y)], 1)
    t.upz[t.z] = mm(flat_y, t.qc[...], NT)


def lower_levels(t):
    flat_y = jnp.concatenate([t.upy[k] for k in range(Y)], 1)
    t.pre[...] = mm(flat_y, t.m0[...].reshape(Y * R, R), NN)


def finish(t):
    flat_z = jnp.concatenate([t.upz[k] for k in range(Z)], 1)
    down = mm(flat_z, t.mz[...].reshape(Z * R, R), NN) + t.pre[...]
    t.out[...] = mm(down, t.wd[...], NN) + t.far8[...]


def vm(*s):
    return pltpu.VMEM(s, F32)


SCRATCH = dict(
    pts=vm(3, EXT * LEAF),
    cols_s=vm(EXT, 3, LEAF, 128),
    lhs8=vm(2 * COLS, EXT * LEAF),
    rh=vm(COLS, EXT * LEAF),
    nodes=vm(3, 3, LV, R),
    mom=vm(COLS, EXT * R),
    basis=vm(8, LV, 8, LEAF),
    lt=vm(LV, R, R),
    mask=pltpu.VMEM((LV, SLOTS), jnp.int32),
    wn=vm(LV, SLOTS),
    fw=vm(EXT, LV * R),
    slab=vm(R, R, 252),
    turned=vm(R * 256, R),
    nslab=vm(3, R, 254),
    nturned=vm(3, 256, R),
    upy=vm(Y, COLS, R),
    upz=vm(Z, COLS, R),
    m0=vm(Y, R, R),
    mz=vm(Z, R, R),
    ltc=vm(R, LV * R),
    qc=vm(R, Y * R),
    wd=vm(R, LV * LEAF),
    pre=vm(COLS, R),
    far8=vm(COLS, LV * LEAF),
)

DMA = pltpu.SemaphoreType.DMA
SEMS = dict(
    lsem=DMA((8,)),
    bs=DMA((2, 7)),
    hs=DMA((2, 6)),
    ms=DMA((2, 2)),
    ys=DMA((2, Y - 1)),
    zs=DMA((2, Z - 1)),
)


def body(points, rhs, basis_in, nodes_in, lt_in, mask_in, top_t, top_n, out, *rest):
    t = Refs()
    for name, ref in zip([*SCRATCH, *SEMS], rest):
        setattr(t, name, ref)
    t.out = out
    t.n_top = top_t.shape[2]
    c = lax.axis_index("clus")
    r = lax.axis_index("rhs")
    z = c // Y
    y = lax.rem(c, Y)
    t.c, t.z, t.y = c, z, y
    n_clus = Y * Z
    nxt = lax.rem(c + 1, n_clus)
    prv = lax.rem(c + n_clus - 1, n_clus)

    r_peers = [(c, lax.rem(r + k, 8)) for k in range(1, 8)]
    y_peers = [(z * Y + lax.rem(y + k, Y), r) for k in range(1, Y)]
    z_peers = [(lax.rem(z + k, Z) * Y + y, r) for k in range(1, Z)]
    everyone = r_peers + y_peers + z_peers + [(nxt, r), (prv, r)]
    barrier = pltpu.get_barrier_semaphore()
    for p in everyone:
        pl.semaphore_signal(barrier, inc=1, device_id=p, device_id_type=MESH)

    own = pl.ds(HALO, LV * LEAF)
    loads = [
        (top_n, t.nslab),
        (top_t, t.slab),
        (points, t.pts.at[:, own]),
        (rhs, t.rh.at[:, own]),
        (mask_in, t.mask),
        (lt_in, t.lt),
        (nodes_in, t.nodes.at[1]),
        (basis_in, t.basis.at[r]),
    ]
    local = []
    for i, (src, dst) in enumerate(loads):
        cp = pltpu.make_async_copy(src, dst, t.lsem.at[i])
        cp.start()
        local.append(cp)

    def remote(src, dst, sem, i, to):
        cp = pltpu.make_async_remote_copy(
            src_ref=src, dst_ref=dst, send_sem=sem.at[0, i], recv_sem=sem.at[1, i], device_id=to, device_id_type=MESH
        )
        cp.start()
        return cp

    pl.semaphore_wait(barrier, len(everyone))

    sent_b = [remote(basis_in, t.basis.at[r], t.bs, i, p) for i, p in enumerate(r_peers)]
    right = pl.ds(LV * LEAF - HALO, HALO)
    left = pl.ds(0, HALO)
    to_left = pl.ds(0, HALO)
    to_right = pl.ds(HALO + LV * LEAF, HALO)
    sent_h = [
        remote(points.at[:, right], t.pts.at[:, to_left], t.hs, 0, (nxt, r)),
        remote(points.at[:, left], t.pts.at[:, to_right], t.hs, 1, (prv, r)),
        remote(rhs.at[:, right], t.rh.at[:, to_left], t.hs, 2, (nxt, r)),
        remote(rhs.at[:, left], t.rh.at[:, to_right], t.hs, 3, (prv, r)),
        remote(nodes_in, t.nodes.at[0], t.hs, 4, (nxt, r)),
        remote(nodes_in, t.nodes.at[2], t.hs, 5, (prv, r)),
    ]
    for cp in local:
        cp.wait()
    extract(t)
    operators(t)
    gather_transfers(t)
    weights(t)

    for cp in sent_b:
        cp.wait_recv()
    expand(t)
    sent_y = [remote(t.upy.at[y], t.upy.at[y], t.ys, i, p) for i, p in enumerate(y_peers)]
    out_r = pl.ds(LV * R, REACH * R)
    out_l = pl.ds(REACH * R, REACH * R)
    sent_m = [
        remote(t.mom.at[:, out_r], t.mom.at[:, pl.ds(0, REACH * R)], t.ms, 0, (nxt, r)),
        remote(t.mom.at[:, out_l], t.mom.at[:, pl.ds((REACH + LV) * R, REACH * R)], t.ms, 1, (prv, r)),
    ]
    lift_basis(t)
    ahead = jnp.where(z < Z // 2, LV, 0)
    for cp in sent_h:
        cp.wait_recv()
    source_columns(t, 0, EXT)
    near(t, 0, ahead)

    for cp in sent_y:
        cp.wait_recv()
    level_three(t)
    sent_z = [remote(t.upz.at[z], t.upz.at[z], t.zs, i, p) for i, p in enumerate(z_peers)]
    lower_levels(t)
    near(t, ahead, LV - ahead)
    for cp in sent_m:
        cp.wait_recv()
    leaf_far(t)

    for cp in sent_z:
        cp.wait_recv()
    finish(t)
    for cp in sent_b + sent_h + sent_m + sent_y + sent_z:
        cp.wait_send()


def on_device(points, rhs_cols, leaf_basis, leaf_nodes, leaf_transfer, near_mask, top_transfer, top_nodes):
    hbm = pl.BlockSpec(memory_space=pltpu.HBM)
    return pl.pallas_call(
        body,
        out_shape=jax.ShapeDtypeStruct(rhs_cols.shape, F32),
        in_specs=[hbm] * 8,
        out_specs=pl.BlockSpec(memory_space=pltpu.VMEM),
        scratch_shapes=[*SCRATCH.values(), *SEMS.values()],
        compiler_params=pltpu.CompilerParams(
            collective_id=0, has_side_effects=True, vmem_limit_bytes=58 * 1024 * 1024
        ),
        cost_estimate=pl.CostEstimate(flops=10**9, bytes_accessed=4 * 10**6, transcendentals=5 * 10**6),
    )(
        points, rhs_cols, leaf_basis, jnp.transpose(leaf_nodes, (1, 0, 2)), leaf_transfer, near_mask,
        jnp.transpose(top_transfer, (1, 2, 0)), jnp.transpose(top_nodes, (1, 2, 0)),
    )


def solution(mesh):
    return jax.shard_map(
        on_device,
        mesh=mesh,
        in_specs=(
            P(None, "clus"),
            P("rhs", "clus"),
            P("clus", "rhs", None),
            P("clus", None, None),
            P("clus", None, None),
            P("clus", None),
            P(),
            P(),
        ),
        out_specs=P("rhs", "clus"),
        check_vma=False,
    )
```

```python
import functools
import math

import jax
import jax.numpy as jnp
from jax import lax
from jax.experimental import pallas as pl
from jax.experimental.pallas import tpu as pltpu
from jax.sharding import PartitionSpec as P

AMPLITUDE = 0.2
INV_SCALE = 1.0 / (2.0 * 0.15 * 0.15)
COORD = math.sqrt(INV_SCALE * math.log2(math.e))
LOG_AMP = math.log2(AMPLITUDE)

F32 = jnp.float32
BF16 = jnp.bfloat16
MESH = pl.DeviceIdType.MESH

NN = (((1,), (0,)), ((), ()))
NT = (((1,), (1,)), ((), ()))
TN = (((0,), (0,)), ((), ()))

Y = 8
Z = 16
R = 64
LEAF = 256
LV = 8
COLS = 4
REACH = 4
SLOTS = 9
EXT = LV + 2 * REACH
HALO = REACH * LEAF
AHEAD = 3


def split(x):
    hi = x.astype(BF16)
    return hi, (x - hi.astype(F32)).astype(BF16)


def dot(a, b, dims):
    return lax.dot_general(a, b, dims, preferred_element_type=F32)


def mm(a, b, dims):
    ah, al = split(a)
    bh, bl = split(b)
    return dot(ah, bh, dims) + (dot(ah, bl, dims) + dot(al, bh, dims))


def mtn(a, b):
    ah, al = split(a)
    bh, bl = split(b)
    return dot(jnp.concatenate([ah, ah, al], 0), jnp.concatenate([bh, bl, bh], 0), TN)


def rows8(x):
    hi = x.astype(BF16).astype(F32)
    return jnp.concatenate([hi, x - hi], 0)


def fold8(x):
    return x[0:COLS] + x[COLS : 2 * COLS]


def columns(seg):
    return jnp.concatenate([seg, jnp.zeros((5, seg.shape[1]), F32)], 0).T


def gauss(cols, rows):
    d0 = cols[0] - rows[0]
    d1 = cols[1] - rows[1]
    d2 = cols[2] - rows[2]
    return jnp.exp2(LOG_AMP - (d0 * d0 + d1 * d1 + d2 * d2))


class Refs:
    pass


def extract(t):
    def turn(a, _):
        slab = t.slab[a]
        low = slab[:, 0:128].T
        high = jnp.concatenate([slab[:, 128:], jnp.zeros((R, 256 - t.n_top), F32)], 1).T
        t.turned[pl.ds(pl.multiple_of(a * 256, 256), 128), :] = low
        t.turned[pl.ds(pl.multiple_of(a * 256 + 128, 128), 128), :] = high
        return 0

    lax.fori_loop(0, R, turn, 0, unroll=4)
    for k in range(3):
        x = t.nslab[k] * COORD
        t.nturned[k, 0:128] = x[:, 0:128].T
        t.nturned[k, 128:256] = jnp.concatenate([x[:, 128:], jnp.zeros((R, 2), F32)], 1).T


def operators(t):
    z, y, c = t.z, t.y, t.c

    def top(n):
        return t.turned[pl.ds(n, R, stride=256), :]

    t0 = lambda k: top(Y * z + k)
    t1 = lambda k: top(128 + 4 * z + k)
    t2 = lambda k: top(192 + 2 * z + k)
    t3 = lambda k: top(224 + k)
    t4 = lambda k: top(240 + k)
    t5 = lambda k: top(248 + k)
    q1 = [mm(t1(k), jnp.concatenate([t0(2 * k), t0(2 * k + 1)], 1), NN) for k in range(4)]
    t.qc[...] = jnp.concatenate(
        [mm(t2(k), jnp.concatenate([q1[2 * k], q1[2 * k + 1]], 1), NN) for k in range(2)], 1
    )
    path = [t0(y), t1(y >> 1), t2(y >> 2), t3(z), t4(z >> 1), t5(z >> 2)]
    e = None
    g_b = []
    for b in range(7):
        off = 256 - 2 * (128 >> b)
        at = off + (c >> b)
        sib = off + ((c >> b) ^ 1)
        mn = [t.nturned[k, pl.ds(at, 1)] for k in range(3)]
        sn = jnp.concatenate([t.nturned[k, pl.ds(sib, 1)] for k in range(3)], 0)
        sc = columns(jnp.concatenate([sn, sn], 1))[0:R]
        s_t = gauss([sc[:, k : k + 1] for k in range(3)], mn)
        if b == 0:
            g_b.append(s_t)
        else:
            e = path[0] if b == 1 else mm(path[b - 1], e, NN)
            g_b.append(mm(s_t, e, NN))
    zero = jnp.zeros((R, R), F32)
    m0, mz = t.m0, t.mz
    m0[y] = zero
    m0[y ^ 1] = g_b[0]
    s1 = (y >> 1) ^ 1
    for k in range(2):
        m0[2 * s1 + k] = mtn(t0(2 * s1 + k), g_b[1])
    s2 = (y >> 2) ^ 1
    for k in range(2):
        half = mtn(t1(2 * s2 + k), g_b[2])
        for j in range(2):
            m0[4 * s2 + 2 * k + j] = mtn(t0(4 * s2 + 2 * k + j), half)
    mz[z] = zero
    mz[z ^ 1] = g_b[3]
    s4 = (z >> 1) ^ 1
    for k in range(2):
        mz[2 * s4 + k] = mtn(t3(2 * s4 + k), g_b[4])
    s5 = (z >> 2) ^ 1
    for k in range(2):
        half = mtn(t4(2 * s5 + k), g_b[5])
        for j in range(2):
            mz[4 * s5 + 2 * k + j] = mtn(t3(4 * s5 + 2 * k + j), half)
    s6 = (z >> 3) ^ 1
    for i in range(2):
        up = mtn(t5(2 * s6 + i), g_b[6])
        for k in range(2):
            half = mtn(t4(4 * s6 + 2 * i + k), up)
            for j in range(2):
                mz[8 * s6 + 4 * i + 2 * k + j] = mtn(t3(8 * s6 + 4 * i + 2 * k + j), half)


def leaf_basis_of(t, g):
    return t.basis[:, g].reshape(R, LEAF)


def gather_transfers(t):
    t.ltc[...] = jnp.concatenate([t.lt[g] for g in range(LV)], 1)


def expand(t):
    parts = []
    for g in range(LV):
        parts.append(mm(t.rh[:, HALO + g * LEAF : HALO + (g + 1) * LEAF], leaf_basis_of(t, g), NT))
    moments = jnp.concatenate(parts, 1)
    t.mom[:, REACH * R : (REACH + LV) * R] = moments
    t.upy[t.y] = mm(moments, t.ltc[...], NT)


def lift_basis(t):
    for g in range(LV):
        t.wd[:, g * LEAF : (g + 1) * LEAF] = mm(t.lt[g], leaf_basis_of(t, g), NN)


def weights(t):
    lane = lax.broadcasted_iota(jnp.int32, (LV, SLOTS), 1)
    row = lax.broadcasted_iota(jnp.int32, (LV, SLOTS), 0)
    place = t.c * LV + row + lane - REACH
    valid = jnp.where((place >= 0) & (place < Y * Z * LV), 1.0, 0.0).astype(F32)
    w = jnp.where(lane == REACH, 1.0, t.mask[...].astype(F32))
    t.wn[...] = w * valid
    wf = (1.0 - w) * valid
    skew = []
    for g in range(LV):
        piece = [wf[g : g + 1]]
        if g > 0:
            piece.insert(0, jnp.zeros((1, g), F32))
        if g < LV - 1:
            piece.append(jnp.zeros((1, LV - 1 - g), F32))
        skew.append(jnp.concatenate(piece, 1))
    skewed = jnp.concatenate(skew, 0)
    spread = jnp.where(
        lax.broadcasted_iota(jnp.int32, (LV, LV * R), 1) // R == lax.broadcasted_iota(jnp.int32, (LV, LV * R), 0),
        1.0, 0.0,
    ).astype(F32)
    t.fw[...] = dot(skewed, spread, TN)


def leaf_far(t):
    m8 = rows8(t.mom[...]).astype(BF16)
    flat = []
    for k in range(3):
        rows = [t.nodes[0, k, l : l + 1] for l in range(LV - REACH, LV)]
        rows += [t.nodes[1, k, l : l + 1] for l in range(LV)]
        rows += [t.nodes[2, k, l : l + 1] for l in range(REACH)]
        flat.append(jnp.concatenate(rows, 1))
    flat_n = jnp.concatenate(flat, 0) * COORD
    mine_n = flat_n[:, REACH * R : (REACH + LV) * R]
    targets = [mine_n[k : k + 1] for k in range(3)]
    far_w = t.fw[...]
    acc = jnp.zeros((2 * COLS, LV * R), F32)
    for q in range(EXT // 4):
        hs, ls = [], []
        for p in range(2):
            cc = columns(flat_n[:, (2 * q + p) * 128 : (2 * q + p + 1) * 128])
            for u in range(2):
                l = 4 * q + 2 * p + u
                part = cc[u * R : (u + 1) * R]
                block = gauss([part[:, k : k + 1] for k in range(3)], targets) * far_w[l : l + 1]
                h, lo = split(block)
                hs.append(h)
                ls.append(lo)
        a = m8[:, q * 256 : (q + 1) * 256]
        acc = acc + dot(a, jnp.concatenate(hs, 0), NN) + dot(a, jnp.concatenate(ls, 0), NN)
    local_far = fold8(acc)
    for g in range(LV):
        cut = slice(g * LEAF, (g + 1) * LEAF)
        t.far8[:, cut] = t.far8[:, cut] + mm(local_far[:, g * R : (g + 1) * R], leaf_basis_of(t, g), NN)


def three(x):
    h = x.astype(BF16).astype(F32)
    m = (x - h).astype(BF16).astype(F32)
    return h, m, (x - h - m).astype(BF16).astype(F32)


def sources(t, first, count):
    def prepare(l, _):
        at = pl.multiple_of(l * LEAF, LEAF)
        x = (t.pts[:, pl.ds(at, LEAF)] - 0.5) * COORD
        h, m, lo = three(x)
        sq = x * x
        n = sq[0:1] + sq[1:2] + sq[2:3]
        one = jnp.ones((3, LEAF), F32)
        rows = jnp.concatenate([h, h, m, h, lo, m, *[-v for v in three(n)], one, jnp.zeros((8, LEAF), F32)], 0)
        for u in range(2):
            t.a_s[pl.ds(pl.multiple_of(at + u * 128, 128), 128), :] = rows[:, u * 128 : (u + 1) * 128].T.astype(BF16)
        t.b_s[:, pl.ds(at, LEAF)] = jnp.concatenate(
            [h, m, h, lo, h, m, 0.5 * one, *[0.5 * v for v in three(LOG_AMP - n)], jnp.zeros((8, LEAF), F32)], 0
        ).astype(BF16) * 2
        t.lhs8[:, pl.ds(at, LEAF)] = rows8(t.rh[:, pl.ds(at, LEAF)])
        return 0

    lax.fori_loop(first, first + count, prepare, 0)


def near(t, first, count):
    def leaf(g, _):
        b = t.b_s[:, pl.ds(pl.multiple_of(HALO + g * LEAF, LEAF), LEAF)]
        wrow = t.wn[pl.ds(g, 1), :]
        acc = jnp.zeros((2 * COLS, LEAF), F32)
        for s in range(SLOTS):
            at = pl.multiple_of((g + s) * LEAF, LEAF)
            a = (t.lhs8[:, pl.ds(at, LEAF)] * wrow[:, s : s + 1]).astype(BF16)
            k_hi, k_lo = split(jnp.exp2(dot(t.a_s[pl.ds(at, LEAF), :], b, NN)))
            acc = acc + dot(a, k_hi, NN) + dot(a, k_lo, NN)
        to = pl.multiple_of(g * LEAF, LEAF)
        t.far8[:, pl.ds(to, LEAF)] = fold8(acc)
        return 0

    lax.fori_loop(first, first + count, leaf, 0)


def level_three(t):
    flat_y = jnp.concatenate([t.upy[k] for k in range(Y)], 1)
    t.upz[t.z] = mm(flat_y, t.qc[...], NT)


def lower_levels(t):
    flat_y = jnp.concatenate([t.upy[k] for k in range(Y)], 1)
    t.pre[...] = mm(flat_y, t.m0[...].reshape(Y * R, R), NN)


def finish(t):
    flat_z = jnp.concatenate([t.upz[k] for k in range(Z)], 1)
    down = mm(flat_z, t.mz[...].reshape(Z * R, R), NN) + t.pre[...]
    t.out[...] = mm(down, t.wd[...], NN) + t.far8[...]


def vm(*s):
    return pltpu.VMEM(s, F32)


SCRATCH = dict(
    pts=vm(3, EXT * LEAF),
    a_s=pltpu.VMEM((EXT * LEAF, 32), BF16),
    b_s=pltpu.VMEM((32, EXT * LEAF), BF16),
    lhs8=vm(2 * COLS, EXT * LEAF),
    rh=vm(COLS, EXT * LEAF),
    nodes=vm(3, 3, LV, R),
    mom=vm(COLS, EXT * R),
    basis=vm(8, LV, 8, LEAF),
    lt=vm(LV, R, R),
    mask=pltpu.VMEM((LV, SLOTS), jnp.int32),
    wn=vm(LV, SLOTS),
    fw=vm(EXT, LV * R),
    slab=vm(R, R, 252),
    turned=vm(R * 256, R),
    nslab=vm(3, R, 254),
    nturned=vm(3, 256, R),
    upy=vm(Y, COLS, R),
    upz=vm(Z, COLS, R),
    m0=vm(Y, R, R),
    mz=vm(Z, R, R),
    ltc=vm(R, LV * R),
    qc=vm(R, Y * R),
    wd=vm(R, LV * LEAF),
    pre=vm(COLS, R),
    far8=vm(COLS, LV * LEAF),
)

DMA = pltpu.SemaphoreType.DMA
SEMS = dict(
    lsem=DMA((8,)),
    bs=DMA((2, 7)),
    hs=DMA((2, 6)),
    ms=DMA((2, 2)),
    ys=DMA((2, Y - 1)),
    zs=DMA((2, Z - 1)),
    known=pltpu.SemaphoreType.REGULAR((3,)),
)


def body(points, rhs, basis_in, nodes_in, lt_in, mask_in, top_t, top_n, out, *rest):
    t = Refs()
    for name, ref in zip([*SCRATCH, *SEMS], rest):
        setattr(t, name, ref)
    t.out = out
    t.n_top = top_t.shape[2]
    c = lax.axis_index("clus")
    r = lax.axis_index("rhs")
    z = c // Y
    y = lax.rem(c, Y)
    t.c, t.z, t.y = c, z, y
    n_clus = Y * Z
    nxt = lax.rem(c + 1, n_clus)
    prv = lax.rem(c + n_clus - 1, n_clus)

    r_peers = [(c, lax.rem(r + k, 8)) for k in range(1, 8)]
    y_at = lambda k: (z * Y + lax.rem(y + Y + k, Y), r)
    z_at = lambda k: (lax.rem(z + Z + k, Z) * Y + y, r)
    y_peers = [y_at(k) for k in range(1, Y)]
    z_peers = [z_at(k) for k in range(1, Z)]

    def signal(sem, p):
        pl.semaphore_signal(sem, inc=1, device_id=p, device_id_type=MESH)

    neighbours = r_peers + [y_at(1), y_at(-1), z_at(1), z_at(-1), (nxt, r), (prv, r)]
    barrier = pltpu.get_barrier_semaphore()
    for p in neighbours:
        signal(barrier, p)

    own = pl.ds(HALO, LV * LEAF)
    loads = [
        (top_n, t.nslab),
        (top_t, t.slab),
        (points, t.pts.at[:, own]),
        (rhs, t.rh.at[:, own]),
        (mask_in, t.mask),
        (lt_in, t.lt),
        (nodes_in, t.nodes.at[1]),
        (basis_in, t.basis.at[r]),
    ]
    local = []
    for i, (src, dst) in enumerate(loads):
        cp = pltpu.make_async_copy(src, dst, t.lsem.at[i])
        cp.start()
        local.append(cp)

    def remote(src, dst, sem, i, to):
        cp = pltpu.make_async_remote_copy(
            src_ref=src, dst_ref=dst, send_sem=sem.at[0, i], recv_sem=sem.at[1, i], device_id=to, device_id_type=MESH
        )
        cp.start()
        return cp

    pl.semaphore_wait(barrier, len(neighbours))

    sent_b = [remote(basis_in, t.basis.at[r], t.bs, i, p) for i, p in enumerate(r_peers)]
    right = pl.ds(LV * LEAF - HALO, HALO)
    left = pl.ds(0, HALO)
    to_left = pl.ds(0, HALO)
    to_right = pl.ds(HALO + LV * LEAF, HALO)
    sent_h = [
        remote(points.at[:, right], t.pts.at[:, to_left], t.hs, 0, (nxt, r)),
        remote(points.at[:, left], t.pts.at[:, to_right], t.hs, 1, (prv, r)),
        remote(rhs.at[:, right], t.rh.at[:, to_left], t.hs, 2, (nxt, r)),
        remote(rhs.at[:, left], t.rh.at[:, to_right], t.hs, 3, (prv, r)),
        remote(nodes_in, t.nodes.at[0], t.hs, 4, (nxt, r)),
        remote(nodes_in, t.nodes.at[2], t.hs, 5, (prv, r)),
    ]
    for p in (y_at(1), y_at(-1), z_at(1), z_at(-1)):
        signal(t.known.at[0], p)
    for cp in local:
        cp.wait()
    extract(t)
    pl.semaphore_wait(t.known.at[0], 4)
    for p in (y_at(2), y_at(-2), z_at(2), z_at(-2)):
        signal(t.known.at[1], p)
    operators(t)
    pl.semaphore_wait(t.known.at[1], 4)
    for p in (z_at(4), z_at(-4)):
        signal(t.known.at[2], p)
    gather_transfers(t)
    weights(t)

    for cp in sent_b:
        cp.wait_recv()
    expand(t)
    sent_y = [remote(t.upy.at[y], t.upy.at[y], t.ys, i, p) for i, p in enumerate(y_peers)]
    out_r = pl.ds(LV * R, REACH * R)
    out_l = pl.ds(REACH * R, REACH * R)
    sent_m = [
        remote(t.mom.at[:, out_r], t.mom.at[:, pl.ds(0, REACH * R)], t.ms, 0, (nxt, r)),
        remote(t.mom.at[:, out_l], t.mom.at[:, pl.ds((REACH + LV) * R, REACH * R)], t.ms, 1, (prv, r)),
    ]
    lift_basis(t)
    for cp in sent_h:
        cp.wait_recv()
    sources(t, 0, EXT)
    near(t, 0, AHEAD)

    pl.semaphore_wait(t.known.at[2], 2)
    for cp in sent_y:
        cp.wait_recv()
    level_three(t)
    sent_z = [remote(t.upz.at[z], t.upz.at[z], t.zs, i, p) for i, p in enumerate(z_peers)]
    lower_levels(t)
    near(t, AHEAD, LV - AHEAD)
    for cp in sent_m:
        cp.wait_recv()
    leaf_far(t)

    for cp in sent_z:
        cp.wait_recv()
    finish(t)
    for cp in sent_b + sent_h + sent_m + sent_y + sent_z:
        cp.wait_send()


def on_device(points, rhs_cols, leaf_basis, leaf_nodes, leaf_transfer, near_mask, top_transfer, top_nodes):
    hbm = pl.BlockSpec(memory_space=pltpu.HBM)
    return pl.pallas_call(
        body,
        out_shape=jax.ShapeDtypeStruct(rhs_cols.shape, F32),
        in_specs=[hbm] * 8,
        out_specs=pl.BlockSpec(memory_space=pltpu.VMEM),
        scratch_shapes=[*SCRATCH.values(), *SEMS.values()],
        compiler_params=pltpu.CompilerParams(
            collective_id=0, has_side_effects=True, vmem_limit_bytes=58 * 1024 * 1024
        ),
        cost_estimate=pl.CostEstimate(flops=10**9, bytes_accessed=4 * 10**6, transcendentals=5 * 10**6),
    )(
        points, rhs_cols, leaf_basis, jnp.transpose(leaf_nodes, (1, 0, 2)), leaf_transfer, near_mask,
        jnp.transpose(top_transfer, (1, 2, 0)), jnp.transpose(top_nodes, (1, 2, 0)),
    )


def solution(mesh):
    return jax.shard_map(
        on_device,
        mesh=mesh,
        in_specs=(
            P(None, "clus"),
            P("rhs", "clus"),
            P("clus", "rhs", None),
            P("clus", None, None),
            P("clus", None, None),
            P("clus", None),
            P(),
            P(),
        ),
        out_specs=P("rhs", "clus"),
        check_vma=False,
    )
```

```python
import functools
import math

import jax
import jax.numpy as jnp
from jax import lax
from jax.experimental import pallas as pl
from jax.experimental.pallas import tpu as pltpu
from jax.sharding import PartitionSpec as P

AMPLITUDE = 0.2
INV_SCALE = 1.0 / (2.0 * 0.15 * 0.15)
COORD = math.sqrt(INV_SCALE * math.log2(math.e))
LOG_AMP = math.log2(AMPLITUDE)

F32 = jnp.float32
BF16 = jnp.bfloat16
MESH = pl.DeviceIdType.MESH

NN = (((1,), (0,)), ((), ()))
NT = (((1,), (1,)), ((), ()))
TN = (((0,), (0,)), ((), ()))

Y = 8
Z = 16
R = 64
LEAF = 256
LV = 8
COLS = 4
REACH = 4
SLOTS = 9
EXT = LV + 2 * REACH
HALO = REACH * LEAF


def split(x):
    hi = x.astype(BF16)
    return hi, (x - hi.astype(F32)).astype(BF16)


def dot(a, b, dims):
    return lax.dot_general(a, b, dims, preferred_element_type=F32)


def mm(a, b, dims):
    ah, al = split(a)
    bh, bl = split(b)
    return dot(ah, bh, dims) + (dot(ah, bl, dims) + dot(al, bh, dims))


def mtn(a, b):
    ah, al = split(a)
    bh, bl = split(b)
    return dot(jnp.concatenate([ah, ah, al], 0), jnp.concatenate([bh, bl, bh], 0), TN)


def rows8(x):
    hi = x.astype(BF16).astype(F32)
    return jnp.concatenate([hi, x - hi], 0)


def fold8(x):
    return x[0:COLS] + x[COLS : 2 * COLS]


def columns(seg):
    return jnp.concatenate([seg, jnp.zeros((5, seg.shape[1]), F32)], 0).T


def gauss(cols, rows):
    d0 = cols[0] - rows[0]
    d1 = cols[1] - rows[1]
    d2 = cols[2] - rows[2]
    return jnp.exp2(LOG_AMP - (d0 * d0 + d1 * d1 + d2 * d2))


class Refs:
    pass


def extract(t):
    def turn(a, _):
        slab = t.slab[a]
        low = slab[:, 0:128].T
        high = jnp.concatenate([slab[:, 128:], jnp.zeros((R, 256 - t.n_top), F32)], 1).T
        t.turned[pl.ds(pl.multiple_of(a * 256, 256), 128), :] = low
        t.turned[pl.ds(pl.multiple_of(a * 256 + 128, 128), 128), :] = high
        return 0

    lax.fori_loop(0, R, turn, 0, unroll=4)
    for k in range(3):
        x = t.nslab[k] * COORD
        t.nturned[k, 0:128] = x[:, 0:128].T
        t.nturned[k, 128:256] = jnp.concatenate([x[:, 128:], jnp.zeros((R, 2), F32)], 1).T


def transfers(t):
    def at(first):
        return lambda k: t.turned[pl.ds(first + k, R, stride=256), :]

    return at(Y * t.z), at(128 + 4 * t.z), at(192 + 2 * t.z), at(224), at(240), at(248)


def upward(t):
    t0, t1, t2 = transfers(t)[:3]
    q1 = [mm(t1(k), jnp.concatenate([t0(2 * k), t0(2 * k + 1)], 1), NN) for k in range(4)]
    t.qc[...] = jnp.concatenate(
        [mm(t2(k), jnp.concatenate([q1[2 * k], q1[2 * k + 1]], 1), NN) for k in range(2)], 1
    )


def downward(t):
    z, y, c = t.z, t.y, t.c
    t0, t1, t2, t3, t4, t5 = transfers(t)
    path = [t0(y), t1(y >> 1), t2(y >> 2), t3(z), t4(z >> 1), t5(z >> 2)]
    e = None
    g_b = []
    for b in range(7):
        off = 256 - 2 * (128 >> b)
        at = off + (c >> b)
        sib = off + ((c >> b) ^ 1)
        mn = [t.nturned[k, pl.ds(at, 1)] for k in range(3)]
        sn = jnp.concatenate([t.nturned[k, pl.ds(sib, 1)] for k in range(3)], 0)
        sc = columns(jnp.concatenate([sn, sn], 1))[0:R]
        s_t = gauss([sc[:, k : k + 1] for k in range(3)], mn)
        if b == 0:
            g_b.append(s_t)
        else:
            e = path[0] if b == 1 else mm(path[b - 1], e, NN)
            g_b.append(mm(s_t, e, NN))
    zero = jnp.zeros((R, R), F32)
    m0, mz = t.m0, t.mz
    m0[y] = zero
    m0[y ^ 1] = g_b[0]
    s1 = (y >> 1) ^ 1
    for k in range(2):
        m0[2 * s1 + k] = mtn(t0(2 * s1 + k), g_b[1])
    s2 = (y >> 2) ^ 1
    for k in range(2):
        half = mtn(t1(2 * s2 + k), g_b[2])
        for j in range(2):
            m0[4 * s2 + 2 * k + j] = mtn(t0(4 * s2 + 2 * k + j), half)
    mz[z] = zero
    mz[z ^ 1] = g_b[3]
    s4 = (z >> 1) ^ 1
    for k in range(2):
        mz[2 * s4 + k] = mtn(t3(2 * s4 + k), g_b[4])
    s5 = (z >> 2) ^ 1
    for k in range(2):
        half = mtn(t4(2 * s5 + k), g_b[5])
        for j in range(2):
            mz[4 * s5 + 2 * k + j] = mtn(t3(4 * s5 + 2 * k + j), half)
    s6 = (z >> 3) ^ 1
    for i in range(2):
        up = mtn(t5(2 * s6 + i), g_b[6])
        for k in range(2):
            half = mtn(t4(4 * s6 + 2 * i + k), up)
            for j in range(2):
                mz[8 * s6 + 4 * i + 2 * k + j] = mtn(t3(8 * s6 + 4 * i + 2 * k + j), half)


def leaf_basis_of(t, g):
    return t.basis[:, :, g].reshape(R, LEAF)


def turn_transfers(t):
    for g in range(0, LV, 2):
        both = jnp.concatenate([t.lt[g], t.lt[g + 1]], 1).T
        t.ltt[g] = both[0:R].reshape(4, 2, 8, R)
        t.ltt[g + 1] = both[R : 2 * R].reshape(4, 2, 8, R)


def half_root(t):
    both = jnp.concatenate([t.rh[:, HALO : HALO + LV * LEAF], t.rh_sib[...]], 0)
    parts = []
    for g in range(LV):
        rows = t.basis[:, pl.ds(t.p, 1), g].reshape(R // 2, LEAF)
        parts.append(mm(both[:, g * LEAF : (g + 1) * LEAF], rows, NT))
    lifted = mm(jnp.concatenate(parts, 1), t.ltt[:, :, pl.ds(t.p, 1)].reshape(LV * R // 2, R), NN)
    t.upy[0, t.y] = lifted[0:COLS]
    t.half[...] = lifted[COLS : 2 * COLS]


def expand(t):
    parts = []
    for g in range(LV):
        parts.append(mm(t.rh[:, HALO + g * LEAF : HALO + (g + 1) * LEAF], leaf_basis_of(t, g), NT))
    t.mom[:, REACH * R : (REACH + LV) * R] = jnp.concatenate(parts, 1)


def lift_basis(t):
    for g in range(LV):
        t.wd[:, g * LEAF : (g + 1) * LEAF] = mm(t.lt[g], leaf_basis_of(t, g), NN)


def weights(t):
    lane = lax.broadcasted_iota(jnp.int32, (LV, SLOTS), 1)
    row = lax.broadcasted_iota(jnp.int32, (LV, SLOTS), 0)
    place = t.c * LV + row + lane - REACH
    valid = jnp.where((place >= 0) & (place < Y * Z * LV), 1.0, 0.0).astype(F32)
    w = jnp.where(lane == REACH, 1.0, t.mask[...].astype(F32))
    t.wn[...] = w * valid
    wf = (1.0 - w) * valid
    skew = []
    for g in range(LV):
        piece = [wf[g : g + 1]]
        if g > 0:
            piece.insert(0, jnp.zeros((1, g), F32))
        if g < LV - 1:
            piece.append(jnp.zeros((1, LV - 1 - g), F32))
        skew.append(jnp.concatenate(piece, 1))
    skewed = jnp.concatenate(skew, 0)
    spread = jnp.where(
        lax.broadcasted_iota(jnp.int32, (LV, LV * R), 1) // R == lax.broadcasted_iota(jnp.int32, (LV, LV * R), 0),
        1.0, 0.0,
    ).astype(F32)
    t.fw[...] = dot(skewed, spread, TN)


def leaf_far(t):
    m8 = rows8(t.mom[...]).astype(BF16)
    flat = []
    for k in range(3):
        rows = [t.nodes[0, k, l : l + 1] for l in range(LV - REACH, LV)]
        rows += [t.nodes[1, k, l : l + 1] for l in range(LV)]
        rows += [t.nodes[2, k, l : l + 1] for l in range(REACH)]
        flat.append(jnp.concatenate(rows, 1))
    flat_n = jnp.concatenate(flat, 0) * COORD
    mine_n = flat_n[:, REACH * R : (REACH + LV) * R]
    targets = [mine_n[k : k + 1] for k in range(3)]
    far_w = t.fw[...]
    acc = jnp.zeros((2 * COLS, LV * R), F32)
    for q in range(EXT // 4):
        hs, ls = [], []
        for p in range(2):
            cc = columns(flat_n[:, (2 * q + p) * 128 : (2 * q + p + 1) * 128])
            for u in range(2):
                l = 4 * q + 2 * p + u
                part = cc[u * R : (u + 1) * R]
                block = gauss([part[:, k : k + 1] for k in range(3)], targets) * far_w[l : l + 1]
                h, lo = split(block)
                hs.append(h)
                ls.append(lo)
        a = m8[:, q * 256 : (q + 1) * 256]
        acc = acc + dot(a, jnp.concatenate(hs, 0), NN) + dot(a, jnp.concatenate(ls, 0), NN)
    local_far = fold8(acc)
    for g in range(LV):
        cut = slice(g * LEAF, (g + 1) * LEAF)
        t.far8[:, cut] = t.far8[:, cut] + mm(local_far[:, g * R : (g + 1) * R], leaf_basis_of(t, g), NN)


def three(x):
    h = x.astype(BF16).astype(F32)
    m = (x - h).astype(BF16).astype(F32)
    return h, m, (x - h - m).astype(BF16).astype(F32)


def sources(t, first, count):
    def prepare(l, _):
        at = pl.multiple_of(l * LEAF, LEAF)
        x = (t.pts[:, pl.ds(at, LEAF)] - 0.5) * COORD
        h, m, lo = three(x)
        sq = x * x
        n = sq[0:1] + sq[1:2] + sq[2:3]
        one = jnp.ones((3, LEAF), F32)
        rows = jnp.concatenate([h, h, m, h, lo, m, *[-v for v in three(n)], one, jnp.zeros((8, LEAF), F32)], 0)
        for u in range(2):
            t.a_s[pl.ds(pl.multiple_of(at + u * 128, 128), 128), :] = rows[:, u * 128 : (u + 1) * 128].T.astype(BF16)
        t.b_s[:, pl.ds(at, LEAF)] = jnp.concatenate(
            [h, m, h, lo, h, m, 0.5 * one, *[0.5 * v for v in three(LOG_AMP - n)], jnp.zeros((8, LEAF), F32)], 0
        ).astype(BF16) * 2
        t.lhs8[:, pl.ds(at, LEAF)] = rows8(t.rh[:, pl.ds(at, LEAF)])
        return 0

    lax.fori_loop(first, first + count, prepare, 0)


def near(t, first, count):
    def leaf(g, _):
        b = t.b_s[:, pl.ds(pl.multiple_of(HALO + g * LEAF, LEAF), LEAF)]
        wrow = t.wn[pl.ds(g, 1), :]
        acc = jnp.zeros((2 * COLS, LEAF), F32)
        for s in range(SLOTS):
            at = pl.multiple_of((g + s) * LEAF, LEAF)
            a = (t.lhs8[:, pl.ds(at, LEAF)] * wrow[:, s : s + 1]).astype(BF16)
            k_hi, k_lo = split(jnp.exp2(dot(t.a_s[pl.ds(at, LEAF), :], b, NN)))
            acc = acc + dot(a, k_hi, NN) + dot(a, k_lo, NN)
        to = pl.multiple_of(g * LEAF, LEAF)
        t.far8[:, pl.ds(to, LEAF)] = fold8(acc)
        return 0

    lax.fori_loop(first, first + count, leaf, 0)


def level_three(t):
    flat_y = jnp.concatenate([t.upy[0, k] + t.upy[1, k] for k in range(Y)], 1)
    t.upz[t.z] = mm(flat_y, t.qc[...], NT)


def lower_levels(t):
    flat_y = jnp.concatenate([t.upy[0, k] + t.upy[1, k] for k in range(Y)], 1)
    t.pre[...] = mm(flat_y, t.m0[...].reshape(Y * R, R), NN)


def finish(t):
    flat_z = jnp.concatenate([t.upz[k] for k in range(Z)], 1)
    down = mm(flat_z, t.mz[...].reshape(Z * R, R), NN) + t.pre[...]
    t.out[...] = mm(down, t.wd[...], NN) + t.far8[...]


def vm(*s):
    return pltpu.VMEM(s, F32)


SCRATCH = dict(
    pts=vm(3, EXT * LEAF),
    a_s=pltpu.VMEM((EXT * LEAF, 32), BF16),
    b_s=pltpu.VMEM((32, EXT * LEAF), BF16),
    lhs8=vm(2 * COLS, EXT * LEAF),
    rh=vm(COLS, EXT * LEAF),
    nodes=vm(3, 3, LV, R),
    mom=vm(COLS, EXT * R),
    basis=vm(4, 2, LV, 8, LEAF),
    rh_sib=vm(COLS, LV * LEAF),
    lt=vm(LV, R, R),
    mask=pltpu.VMEM((LV, SLOTS), jnp.int32),
    wn=vm(LV, SLOTS),
    fw=vm(EXT, LV * R),
    slab=vm(R, R, 252),
    turned=vm(R * 256, R),
    nslab=vm(3, R, 254),
    nturned=vm(3, 256, R),
    upy=vm(2, Y, COLS, R),
    half=vm(COLS, R),
    upz=vm(Z, COLS, R),
    m0=vm(Y, R, R),
    mz=vm(Z, R, R),
    ltt=vm(LV, 4, 2, 8, R),
    qc=vm(R, Y * R),
    wd=vm(R, LV * LEAF),
    pre=vm(COLS, R),
    far8=vm(COLS, LV * LEAF),
)

DMA = pltpu.SemaphoreType.DMA
SEMS = dict(
    lsem=DMA((8,)),
    bs=DMA((2, 3)),
    ss=DMA((2, 5)),
    hs=DMA((2, 6)),
    ms=DMA((2, 2)),
    ys=DMA((2, 2 * Y - 1)),
    zs=DMA((2, Z - 1)),
    known=pltpu.SemaphoreType.REGULAR((3,)),
)


def body(points, rhs, basis_in, nodes_in, lt_in, mask_in, top_t, top_n, out, *rest):
    t = Refs()
    for name, ref in zip([*SCRATCH, *SEMS], rest):
        setattr(t, name, ref)
    t.out = out
    t.n_top = top_t.shape[2]
    c = lax.axis_index("clus")
    r = lax.axis_index("rhs")
    z = c // Y
    y = lax.rem(c, Y)
    t.c, t.z, t.y, t.p = c, z, y, lax.rem(r, 2)
    block = r // 2
    other = r + 1 - 2 * t.p
    n_clus = Y * Z
    nxt = lax.rem(c + 1, n_clus)
    prv = lax.rem(c + n_clus - 1, n_clus)

    r_peers = [(c, lax.rem(r + k, 8)) for k in range(1, 8)]
    y_at = lambda k, core=r: (z * Y + lax.rem(y + Y + k, Y), core)
    z_at = lambda k: (lax.rem(z + Z + k, Z) * Y + y, r)
    x_peers = r_peers[1::2]
    y_peers = [y_at(k) for k in range(1, Y)]
    y_others = [y_at(k, other) for k in range(Y)]
    z_peers = [z_at(k) for k in range(1, Z)]

    def signal(sem, p):
        pl.semaphore_signal(sem, inc=1, device_id=p, device_id_type=MESH)

    rank = lax.rem(z + Z - 1, Z)
    neighbours = r_peers + [y_at(1), y_at(-1), y_at(1, other), y_at(-1, other), (nxt, r), (prv, r)]
    barrier = pltpu.get_barrier_semaphore()
    for p in neighbours:
        signal(barrier, p)
    for k in range(1, Z):

        @pl.when(rank + k < Z)
        def _(k=k):
            signal(barrier, z_at(k))

    own = pl.ds(HALO, LV * LEAF)
    loads = [
        (top_n, t.nslab),
        (top_t, t.slab),
        (points, t.pts.at[:, own]),
        (rhs, t.rh.at[:, own]),
        (mask_in, t.mask),
        (lt_in, t.lt),
        (nodes_in, t.nodes.at[1]),
        (basis_in, t.basis.at[block, t.p]),
    ]
    local = []
    for i, (src, dst) in enumerate(loads):
        cp = pltpu.make_async_copy(src, dst, t.lsem.at[i])
        cp.start()
        local.append(cp)

    def remote(src, dst, sem, i, to):
        cp = pltpu.make_async_remote_copy(
            src_ref=src, dst_ref=dst, send_sem=sem.at[0, i], recv_sem=sem.at[1, i], device_id=to, device_id_type=MESH
        )
        cp.start()
        return cp

    early = (z == 0) & ((c > 0) | (r > 0))

    def alone():
        for cp in local:
            cp.wait()
        extract(t)
        upward(t)
        turn_transfers(t)
        weights(t)

    @pl.when(early)
    def _():
        alone()
        downward(t)

    pl.semaphore_wait(barrier, len(neighbours) + rank)

    mine = t.basis.at[block, t.p]
    sent_b = [remote(basis_in, mine, t.bs, i, p) for i, p in enumerate(x_peers)]
    sent_r = [remote(rhs, t.rh_sib, t.ss, 0, (c, other))]
    sent_s = [remote(basis_in, mine, t.ss, 1, (c, other))]
    right = pl.ds(LV * LEAF - HALO, HALO)
    left = pl.ds(0, HALO)
    to_left = pl.ds(0, HALO)
    to_right = pl.ds(HALO + LV * LEAF, HALO)
    sent_h = [
        remote(points.at[:, right], t.pts.at[:, to_left], t.hs, 0, (nxt, r)),
        remote(points.at[:, left], t.pts.at[:, to_right], t.hs, 1, (prv, r)),
        remote(rhs.at[:, right], t.rh.at[:, to_left], t.hs, 2, (nxt, r)),
        remote(rhs.at[:, left], t.rh.at[:, to_right], t.hs, 3, (prv, r)),
        remote(nodes_in, t.nodes.at[0], t.hs, 4, (nxt, r)),
        remote(nodes_in, t.nodes.at[2], t.hs, 5, (prv, r)),
    ]
    for p in (y_at(1), y_at(-1)):
        signal(t.known.at[0], p)
    for k in range(1, Z):

        @pl.when(rank - k >= 0)
        def _(k=k):
            signal(t.known.at[2], z_at(-k))

    @pl.when(jnp.logical_not(early))
    def _():
        alone()

    pl.semaphore_wait(t.known.at[0], 2)
    for p in (y_at(2), y_at(-2)):
        signal(t.known.at[1], p)
    for cp in sent_h:
        cp.wait_recv()
    ready = jnp.where(early, EXT, 0)
    first = jnp.where(early, 1, 0)
    second = jnp.where(early, 5, 0)
    sources(t, 0, ready)
    near(t, 0, first)
    pl.semaphore_wait(t.known.at[1], 2)

    for cp in sent_b + sent_r:
        cp.wait_recv()
    half_root(t)
    sent_y = [remote(t.upy.at[0, y], t.upy.at[0, y], t.ys, i, p) for i, p in enumerate(y_peers)]
    sent_y += [remote(t.half, t.upy.at[1, y], t.ys, Y - 1 + i, p) for i, p in enumerate(y_others)]
    for k in range(1, 4):
        there = t.basis.at[lax.rem(block + k, 4), t.p]
        sent_s.append(remote(there, there, t.ss, 1 + k, (c, other)))

    @pl.when(jnp.logical_not(early))
    def _():
        downward(t)

    for cp in sent_s:
        cp.wait_recv()
    expand(t)
    out_r = pl.ds(LV * R, REACH * R)
    out_l = pl.ds(REACH * R, REACH * R)
    sent_m = [
        remote(t.mom.at[:, out_r], t.mom.at[:, pl.ds(0, REACH * R)], t.ms, 0, (nxt, r)),
        remote(t.mom.at[:, out_l], t.mom.at[:, pl.ds((REACH + LV) * R, REACH * R)], t.ms, 1, (prv, r)),
    ]
    lift_basis(t)
    sources(t, ready, EXT - ready)
    near(t, first, second - first)


    @pl.when(rank < Z - 1)
    def _():
        pl.semaphore_wait(t.known.at[2], Z - 1 - rank)

    for cp in sent_y:
        cp.wait_recv()
    level_three(t)
    sent_z = [remote(t.upz.at[z], t.upz.at[z], t.zs, i, p) for i, p in enumerate(z_peers)]
    lower_levels(t)
    near(t, second, LV - second)
    for cp in sent_m:
        cp.wait_recv()
    leaf_far(t)

    for cp in sent_z:
        cp.wait_recv()
    finish(t)
    for cp in sent_b + sent_r + sent_s + sent_h + sent_m + sent_y + sent_z:
        cp.wait_send()


def on_device(points, rhs_cols, leaf_basis, leaf_nodes, leaf_transfer, near_mask, top_transfer, top_nodes):
    hbm = pl.BlockSpec(memory_space=pltpu.HBM)
    return pl.pallas_call(
        body,
        out_shape=jax.ShapeDtypeStruct(rhs_cols.shape, F32),
        in_specs=[hbm] * 8,
        out_specs=pl.BlockSpec(memory_space=pltpu.VMEM),
        scratch_shapes=[*SCRATCH.values(), *SEMS.values()],
        compiler_params=pltpu.CompilerParams(
            collective_id=0, has_side_effects=True, vmem_limit_bytes=58 * 1024 * 1024
        ),
        cost_estimate=pl.CostEstimate(flops=10**9, bytes_accessed=4 * 10**6, transcendentals=5 * 10**6),
    )(
        points, rhs_cols, leaf_basis, jnp.transpose(leaf_nodes, (1, 0, 2)), leaf_transfer, near_mask,
        jnp.transpose(top_transfer, (1, 2, 0)), jnp.transpose(top_nodes, (1, 2, 0)),
    )


def solution(mesh):
    return jax.shard_map(
        on_device,
        mesh=mesh,
        in_specs=(
            P(None, "clus"),
            P("rhs", "clus"),
            P("clus", "rhs", None),
            P("clus", None, None),
            P("clus", None, None),
            P("clus", None),
            P(),
            P(),
        ),
        out_specs=P("rhs", "clus"),
        check_vma=False,
    )
```

```python
import functools
import math

import jax
import jax.numpy as jnp
from jax import lax
from jax.experimental import pallas as pl
from jax.experimental.pallas import tpu as pltpu
from jax.sharding import PartitionSpec as P

AMPLITUDE = 0.2
INV_SCALE = 1.0 / (2.0 * 0.15 * 0.15)
COORD = math.sqrt(INV_SCALE * math.log2(math.e))
LOG_AMP = math.log2(AMPLITUDE)

F32 = jnp.float32
BF16 = jnp.bfloat16
MESH = pl.DeviceIdType.MESH

NN = (((1,), (0,)), ((), ()))
NT = (((1,), (1,)), ((), ()))
TN = (((0,), (0,)), ((), ()))

Y = 8
Z = 16
R = 64
LEAF = 256
LV = 8
COLS = 4
REACH = 4
SLOTS = 9
EXT = LV + 2 * REACH
HALO = REACH * LEAF


def split(x):
    hi = x.astype(BF16)
    return hi, (x - hi.astype(F32)).astype(BF16)


def dot(a, b, dims):
    return lax.dot_general(a, b, dims, preferred_element_type=F32)


def mm(a, b, dims):
    ah, al = split(a)
    bh, bl = split(b)
    return dot(ah, bh, dims) + (dot(ah, bl, dims) + dot(al, bh, dims))


def mtn(a, b):
    ah, al = split(a)
    bh, bl = split(b)
    return dot(jnp.concatenate([ah, ah, al], 0), jnp.concatenate([bh, bl, bh], 0), TN)


def rows8(x):
    hi = x.astype(BF16).astype(F32)
    return jnp.concatenate([hi, x - hi], 0)


def fold8(x):
    return x[0:COLS] + x[COLS : 2 * COLS]


def columns(seg):
    return jnp.concatenate([seg, jnp.zeros((5, seg.shape[1]), F32)], 0).T


def gauss(cols, rows):
    d0 = cols[0] - rows[0]
    d1 = cols[1] - rows[1]
    d2 = cols[2] - rows[2]
    return jnp.exp2(LOG_AMP - (d0 * d0 + d1 * d1 + d2 * d2))


class Refs:
    pass


def extract(t):
    def turn(a, _):
        slab = t.slab[a]
        low = slab[:, 0:128].T
        high = jnp.concatenate([slab[:, 128:], jnp.zeros((R, 256 - t.n_top), F32)], 1).T
        t.turned[pl.ds(pl.multiple_of(a * 256, 256), 128), :] = low
        t.turned[pl.ds(pl.multiple_of(a * 256 + 128, 128), 128), :] = high
        return 0

    lax.fori_loop(0, R, turn, 0, unroll=4)
    for k in range(3):
        x = t.nslab[k] * COORD
        t.nturned[k, 0:128] = x[:, 0:128].T
        t.nturned[k, 128:256] = jnp.concatenate([x[:, 128:], jnp.zeros((R, 2), F32)], 1).T


def transfers(t):
    def at(first):
        return lambda k: t.turned[pl.ds(first + k, R, stride=256), :]

    return at(Y * t.z), at(128 + 4 * t.z), at(192 + 2 * t.z), at(224), at(240), at(248)


def upward(t):
    t0, t1, t2 = transfers(t)[:3]
    q1 = [mm(t1(k), jnp.concatenate([t0(2 * k), t0(2 * k + 1)], 1), NN) for k in range(4)]
    t.qc[...] = jnp.concatenate(
        [mm(t2(k), jnp.concatenate([q1[2 * k], q1[2 * k + 1]], 1), NN) for k in range(2)], 1
    )


def downward(t):
    z, y, c = t.z, t.y, t.c
    t0, t1, t2, t3, t4, t5 = transfers(t)
    path = [t0(y), t1(y >> 1), t2(y >> 2), t3(z), t4(z >> 1), t5(z >> 2)]
    e = None
    g_b = []
    for b in range(7):
        off = 256 - 2 * (128 >> b)
        at = off + (c >> b)
        sib = off + ((c >> b) ^ 1)
        mn = [t.nturned[k, pl.ds(at, 1)] for k in range(3)]
        sn = jnp.concatenate([t.nturned[k, pl.ds(sib, 1)] for k in range(3)], 0)
        sc = columns(jnp.concatenate([sn, sn], 1))[0:R]
        s_t = gauss([sc[:, k : k + 1] for k in range(3)], mn)
        if b == 0:
            g_b.append(s_t)
        else:
            e = path[0] if b == 1 else mm(path[b - 1], e, NN)
            g_b.append(mm(s_t, e, NN))
    zero = jnp.zeros((R, R), F32)
    m0, mz = t.m0, t.mz
    m0[y] = zero
    m0[y ^ 1] = g_b[0]
    s1 = (y >> 1) ^ 1
    for k in range(2):
        m0[2 * s1 + k] = mtn(t0(2 * s1 + k), g_b[1])
    s2 = (y >> 2) ^ 1
    for k in range(2):
        half = mtn(t1(2 * s2 + k), g_b[2])
        for j in range(2):
            m0[4 * s2 + 2 * k + j] = mtn(t0(4 * s2 + 2 * k + j), half)
    mz[z] = zero
    mz[z ^ 1] = g_b[3]
    s4 = (z >> 1) ^ 1
    for k in range(2):
        mz[2 * s4 + k] = mtn(t3(2 * s4 + k), g_b[4])
    s5 = (z >> 2) ^ 1
    for k in range(2):
        half = mtn(t4(2 * s5 + k), g_b[5])
        for j in range(2):
            mz[4 * s5 + 2 * k + j] = mtn(t3(4 * s5 + 2 * k + j), half)
    s6 = (z >> 3) ^ 1
    for i in range(2):
        up = mtn(t5(2 * s6 + i), g_b[6])
        for k in range(2):
            half = mtn(t4(4 * s6 + 2 * i + k), up)
            for j in range(2):
                mz[8 * s6 + 4 * i + 2 * k + j] = mtn(t3(8 * s6 + 4 * i + 2 * k + j), half)


def leaf_basis_of(t, g):
    return t.basis[:, :, g].reshape(R, LEAF)


def turn_transfers(t):
    for g in range(0, LV, 2):
        both = jnp.concatenate([t.lt[g], t.lt[g + 1]], 1).T
        t.ltt[g] = both[0:R].reshape(4, 2, 8, R)
        t.ltt[g + 1] = both[R : 2 * R].reshape(4, 2, 8, R)


def half_root(t):
    both = jnp.concatenate([t.rh[:, HALO : HALO + LV * LEAF], t.rh_sib[...]], 0)
    parts = []
    for g in range(LV):
        rows = t.basis[:, pl.ds(t.p, 1), g].reshape(R // 2, LEAF)
        parts.append(mm(both[:, g * LEAF : (g + 1) * LEAF], rows, NT))
    lifted = mm(jnp.concatenate(parts, 1), t.ltt[:, :, pl.ds(t.p, 1)].reshape(LV * R // 2, R), NN)
    t.upy[0, t.y] = lifted[0:COLS]
    t.half[...] = lifted[COLS : 2 * COLS]


def expand(t):
    parts = []
    for g in range(LV):
        parts.append(mm(t.rh[:, HALO + g * LEAF : HALO + (g + 1) * LEAF], leaf_basis_of(t, g), NT))
    t.mom[:, REACH * R : (REACH + LV) * R] = jnp.concatenate(parts, 1)


def lift_basis(t):
    for g in range(LV):
        t.wd[:, g * LEAF : (g + 1) * LEAF] = mm(t.lt[g], leaf_basis_of(t, g), NN)


def weights(t):
    lane = lax.broadcasted_iota(jnp.int32, (LV, SLOTS), 1)
    row = lax.broadcasted_iota(jnp.int32, (LV, SLOTS), 0)
    place = t.c * LV + row + lane - REACH
    valid = jnp.where((place >= 0) & (place < Y * Z * LV), 1.0, 0.0).astype(F32)
    w = jnp.where(lane == REACH, 1.0, t.mask[...].astype(F32))
    t.wn[...] = w * valid
    wf = (1.0 - w) * valid
    skew = []
    for g in range(LV):
        piece = [wf[g : g + 1]]
        if g > 0:
            piece.insert(0, jnp.zeros((1, g), F32))
        if g < LV - 1:
            piece.append(jnp.zeros((1, LV - 1 - g), F32))
        skew.append(jnp.concatenate(piece, 1))
    skewed = jnp.concatenate(skew, 0)
    spread = jnp.where(
        lax.broadcasted_iota(jnp.int32, (LV, LV * R), 1) // R == lax.broadcasted_iota(jnp.int32, (LV, LV * R), 0),
        1.0, 0.0,
    ).astype(F32)
    t.fw[...] = dot(skewed, spread, TN)


def leaf_far(t):
    m8 = rows8(t.mom[...]).astype(BF16)
    flat = []
    for k in range(3):
        rows = [t.nodes[0, k, l : l + 1] for l in range(LV - REACH, LV)]
        rows += [t.nodes[1, k, l : l + 1] for l in range(LV)]
        rows += [t.nodes[2, k, l : l + 1] for l in range(REACH)]
        flat.append(jnp.concatenate(rows, 1))
    flat_n = jnp.concatenate(flat, 0) * COORD
    mine_n = flat_n[:, REACH * R : (REACH + LV) * R]
    targets = [mine_n[k : k + 1] for k in range(3)]
    far_w = t.fw[...]
    acc = jnp.zeros((2 * COLS, LV * R), F32)
    for q in range(EXT // 4):
        hs, ls = [], []
        for p in range(2):
            cc = columns(flat_n[:, (2 * q + p) * 128 : (2 * q + p + 1) * 128])
            for u in range(2):
                l = 4 * q + 2 * p + u
                part = cc[u * R : (u + 1) * R]
                block = gauss([part[:, k : k + 1] for k in range(3)], targets) * far_w[l : l + 1]
                h, lo = split(block)
                hs.append(h)
                ls.append(lo)
        a = m8[:, q * 256 : (q + 1) * 256]
        acc = acc + dot(a, jnp.concatenate(hs, 0), NN) + dot(a, jnp.concatenate(ls, 0), NN)
    local_far = fold8(acc)
    for g in range(LV):
        cut = slice(g * LEAF, (g + 1) * LEAF)
        t.far8[:, cut] = t.far8[:, cut] + mm(local_far[:, g * R : (g + 1) * R], leaf_basis_of(t, g), NN)


def three(x):
    h = x.astype(BF16).astype(F32)
    m = (x - h).astype(BF16).astype(F32)
    return h, m, (x - h - m).astype(BF16).astype(F32)


def sources(t, first, count):
    def prepare(l, _):
        at = pl.multiple_of(l * LEAF, LEAF)
        x = (t.pts[:, pl.ds(at, LEAF)] - 0.5) * COORD
        h, m, lo = three(x)
        sq = x * x
        n = sq[0:1] + sq[1:2] + sq[2:3]
        one = jnp.ones((3, LEAF), F32)
        rows = jnp.concatenate([h, h, m, h, lo, m, *[-v for v in three(n)], one, jnp.zeros((8, LEAF), F32)], 0)
        for u in range(2):
            t.a_s[pl.ds(pl.multiple_of(at + u * 128, 128), 128), :] = rows[:, u * 128 : (u + 1) * 128].T.astype(BF16)
        t.b_s[:, pl.ds(at, LEAF)] = jnp.concatenate(
            [h, m, h, lo, h, m, 0.5 * one, *[0.5 * v for v in three(LOG_AMP - n)], jnp.zeros((8, LEAF), F32)], 0
        ).astype(BF16) * 2
        t.lhs8[:, pl.ds(at, LEAF)] = rows8(t.rh[:, pl.ds(at, LEAF)])
        return 0

    lax.fori_loop(first, first + count, prepare, 0)


def near(t, first, count):
    def leaf(g, _):
        b = t.b_s[:, pl.ds(pl.multiple_of(HALO + g * LEAF, LEAF), LEAF)]
        wrow = t.wn[pl.ds(g, 1), :]
        acc = jnp.zeros((2 * COLS, LEAF), F32)
        for s in range(SLOTS):
            at = pl.multiple_of((g + s) * LEAF, LEAF)
            a = (t.lhs8[:, pl.ds(at, LEAF)] * wrow[:, s : s + 1]).astype(BF16)
            k_hi, k_lo = split(jnp.exp2(dot(t.a_s[pl.ds(at, LEAF), :], b, NN)))
            acc = acc + dot(a, k_hi, NN) + dot(a, k_lo, NN)
        to = pl.multiple_of(g * LEAF, LEAF)
        t.far8[:, pl.ds(to, LEAF)] = fold8(acc)
        return 0

    lax.fori_loop(first, first + count, leaf, 0)


def level_three(t):
    flat_y = jnp.concatenate([t.upy[0, k] + t.upy[1, k] for k in range(Y)], 1)
    t.upz[t.z] = mm(flat_y, t.qc[...], NT)


def lower_levels(t):
    flat_y = jnp.concatenate([t.upy[0, k] + t.upy[1, k] for k in range(Y)], 1)
    t.pre[...] = mm(flat_y, t.m0[...].reshape(Y * R, R), NN)


def finish(t):
    flat_z = jnp.concatenate([t.upz[k] for k in range(Z)], 1)
    down = mm(flat_z, t.mz[...].reshape(Z * R, R), NN) + t.pre[...]
    t.out[...] = mm(down, t.wd[...], NN) + t.far8[...]


def vm(*s):
    return pltpu.VMEM(s, F32)


SCRATCH = dict(
    pts=vm(3, EXT * LEAF),
    a_s=pltpu.VMEM((EXT * LEAF, 32), BF16),
    b_s=pltpu.VMEM((32, EXT * LEAF), BF16),
    lhs8=vm(2 * COLS, EXT * LEAF),
    rh=vm(COLS, EXT * LEAF),
    nodes=vm(3, 3, LV, R),
    mom=vm(COLS, EXT * R),
    basis=vm(4, 2, LV, 8, LEAF),
    rh_sib=vm(COLS, LV * LEAF),
    lt=vm(LV, R, R),
    mask=pltpu.VMEM((LV, SLOTS), jnp.int32),
    wn=vm(LV, SLOTS),
    fw=vm(EXT, LV * R),
    slab=vm(R, R, 252),
    turned=vm(R * 256, R),
    nslab=vm(3, R, 254),
    nturned=vm(3, 256, R),
    upy=vm(2, Y, COLS, R),
    half=vm(COLS, R),
    upz=vm(Z, COLS, R),
    m0=vm(Y, R, R),
    mz=vm(Z, R, R),
    ltt=vm(LV, 4, 2, 8, R),
    qc=vm(R, Y * R),
    wd=vm(R, LV * LEAF),
    pre=vm(COLS, R),
    far8=vm(COLS, LV * LEAF),
)

DMA = pltpu.SemaphoreType.DMA
SEMS = dict(
    lsem=DMA((8,)),
    bs=DMA((2, 3)),
    ss=DMA((2, 5)),
    hs=DMA((2, 6)),
    ms=DMA((2, 2)),
    ys=DMA((2, 2 * Y - 1)),
    zs=DMA((2, Z - 1)),
    known=pltpu.SemaphoreType.REGULAR((2,)),
)


def body(points, rhs, basis_in, nodes_in, lt_in, mask_in, top_t, top_n, out, *rest):
    t = Refs()
    for name, ref in zip([*SCRATCH, *SEMS], rest):
        setattr(t, name, ref)
    t.out = out
    t.n_top = top_t.shape[2]
    c = lax.axis_index("clus")
    r = lax.axis_index("rhs")
    z = c // Y
    y = lax.rem(c, Y)
    t.c, t.z, t.y, t.p = c, z, y, lax.rem(r, 2)
    block = r // 2
    other = r + 1 - 2 * t.p
    n_clus = Y * Z
    nxt = lax.rem(c + 1, n_clus)
    prv = lax.rem(c + n_clus - 1, n_clus)

    r_peers = [(c, lax.rem(r + k, 8)) for k in range(1, 8)]
    y_at = lambda k, core=r: (z * Y + lax.rem(y + Y + k, Y), core)
    z_at = lambda k: (lax.rem(z + Z + k, Z) * Y + y, r)
    x_peers = r_peers[1::2]
    y_peers = [y_at(k) for k in range(1, Y)]
    y_others = [y_at(k, other) for k in range(Y)]
    z_peers = [z_at(k) for k in range(1, Z)]

    def signal(sem, p):
        pl.semaphore_signal(sem, inc=1, device_id=p, device_id_type=MESH)

    rank = jnp.where((y == 0) & (r == 0), lax.rem(z + Z - 1, Z), z)
    neighbours = r_peers + [y_at(k, q) for k in (1, -1, 2, -2) for q in (r, other)]
    neighbours += [(nxt, r), (prv, r)]
    barrier = pltpu.get_barrier_semaphore()
    for p in neighbours:
        signal(barrier, p)
    for k in range(1, Z):

        @pl.when(rank + k < Z)
        def _(k=k):
            signal(barrier, z_at(k))

    own = pl.ds(HALO, LV * LEAF)
    loads = [
        (top_n, t.nslab),
        (top_t, t.slab),
        (points, t.pts.at[:, own]),
        (rhs, t.rh.at[:, own]),
        (mask_in, t.mask),
        (lt_in, t.lt),
        (nodes_in, t.nodes.at[1]),
        (basis_in, t.basis.at[block, t.p]),
    ]
    local = []
    for i, (src, dst) in enumerate(loads):
        cp = pltpu.make_async_copy(src, dst, t.lsem.at[i])
        cp.start()
        local.append(cp)

    def remote(src, dst, sem, i, to):
        cp = pltpu.make_async_remote_copy(
            src_ref=src, dst_ref=dst, send_sem=sem.at[0, i], recv_sem=sem.at[1, i], device_id=to, device_id_type=MESH
        )
        cp.start()
        return cp

    early = (z == 0) & ((c > 0) | (r > 0))

    def alone():
        for cp in local:
            cp.wait()
        extract(t)
        upward(t)
        turn_transfers(t)
        weights(t)

    @pl.when(early)
    def _():
        alone()
        downward(t)

    pl.semaphore_wait(barrier, len(neighbours) + rank)

    mine = t.basis.at[block, t.p]
    sent_b = [remote(basis_in, mine, t.bs, i, p) for i, p in enumerate(x_peers)]
    sent_r = [remote(rhs, t.rh_sib, t.ss, 0, (c, other))]
    sent_s = [remote(basis_in, mine, t.ss, 1, (c, other))]
    right = pl.ds(LV * LEAF - HALO, HALO)
    left = pl.ds(0, HALO)
    to_left = pl.ds(0, HALO)
    to_right = pl.ds(HALO + LV * LEAF, HALO)
    sent_h = [
        remote(points.at[:, right], t.pts.at[:, to_left], t.hs, 0, (nxt, r)),
        remote(points.at[:, left], t.pts.at[:, to_right], t.hs, 1, (prv, r)),
        remote(rhs.at[:, right], t.rh.at[:, to_left], t.hs, 2, (nxt, r)),
        remote(rhs.at[:, left], t.rh.at[:, to_right], t.hs, 3, (prv, r)),
        remote(nodes_in, t.nodes.at[0], t.hs, 4, (nxt, r)),
        remote(nodes_in, t.nodes.at[2], t.hs, 5, (prv, r)),
    ]
    for p in (y_at(2), y_at(-2)):
        signal(t.known.at[0], p)
    for k in range(1, Z):

        @pl.when(rank - k >= 0)
        def _(k=k):
            signal(t.known.at[1], z_at(-k))

    @pl.when(jnp.logical_not(early))
    def _():
        alone()

    for cp in sent_h:
        cp.wait_recv()
    ready = jnp.where(early, EXT, 0)
    first = jnp.where(early, 1, 0)
    second = jnp.where(early, 6, 0)
    sources(t, 0, ready)
    near(t, 0, first)
    pl.semaphore_wait(t.known.at[0], 2)

    for cp in sent_b + sent_r:
        cp.wait_recv()
    half_root(t)
    sent_y = [remote(t.upy.at[0, y], t.upy.at[0, y], t.ys, i, p) for i, p in enumerate(y_peers)]
    sent_y += [remote(t.half, t.upy.at[1, y], t.ys, Y - 1 + i, p) for i, p in enumerate(y_others)]
    for k in range(1, 4):
        there = t.basis.at[lax.rem(block + k, 4), t.p]
        sent_s.append(remote(there, there, t.ss, 1 + k, (c, other)))

    @pl.when(jnp.logical_not(early))
    def _():
        downward(t)

    for cp in sent_s:
        cp.wait_recv()
    expand(t)
    out_r = pl.ds(LV * R, REACH * R)
    out_l = pl.ds(REACH * R, REACH * R)
    sent_m = [
        remote(t.mom.at[:, out_r], t.mom.at[:, pl.ds(0, REACH * R)], t.ms, 0, (nxt, r)),
        remote(t.mom.at[:, out_l], t.mom.at[:, pl.ds((REACH + LV) * R, REACH * R)], t.ms, 1, (prv, r)),
    ]
    lift_basis(t)
    middle = jnp.where(z < 4, EXT, 0)
    sources(t, ready, middle - ready)
    near(t, first, second - first)


    @pl.when(rank < Z - 1)
    def _():
        pl.semaphore_wait(t.known.at[1], Z - 1 - rank)

    for cp in sent_y:
        cp.wait_recv()
    level_three(t)
    sent_z = [remote(t.upz.at[z], t.upz.at[z], t.zs, i, p) for i, p in enumerate(z_peers)]
    lower_levels(t)
    sources(t, middle, EXT - middle)
    near(t, second, LV - second)
    for cp in sent_m:
        cp.wait_recv()
    leaf_far(t)

    for cp in sent_z:
        cp.wait_recv()
    finish(t)
    for cp in sent_b + sent_r + sent_s + sent_h + sent_m + sent_y + sent_z:
        cp.wait_send()


def on_device(points, rhs_cols, leaf_basis, leaf_nodes, leaf_transfer, near_mask, top_transfer, top_nodes):
    hbm = pl.BlockSpec(memory_space=pltpu.HBM)
    return pl.pallas_call(
        body,
        out_shape=jax.ShapeDtypeStruct(rhs_cols.shape, F32),
        in_specs=[hbm] * 8,
        out_specs=pl.BlockSpec(memory_space=pltpu.VMEM),
        scratch_shapes=[*SCRATCH.values(), *SEMS.values()],
        compiler_params=pltpu.CompilerParams(
            collective_id=0, has_side_effects=True, vmem_limit_bytes=58 * 1024 * 1024
        ),
        cost_estimate=pl.CostEstimate(flops=10**9, bytes_accessed=4 * 10**6, transcendentals=5 * 10**6),
    )(
        points, rhs_cols, leaf_basis, jnp.transpose(leaf_nodes, (1, 0, 2)), leaf_transfer, near_mask,
        jnp.transpose(top_transfer, (1, 2, 0)), jnp.transpose(top_nodes, (1, 2, 0)),
    )


def solution(mesh):
    return jax.shard_map(
        on_device,
        mesh=mesh,
        in_specs=(
            P(None, "clus"),
            P("rhs", "clus"),
            P("clus", "rhs", None),
            P("clus", None, None),
            P("clus", None, None),
            P("clus", None),
            P(),
            P(),
        ),
        out_specs=P("rhs", "clus"),
        check_vma=False,
    )
```
